256 devices in a mesh: wide: 32 (over y, z), narrow: 8 (over x, core).
Axes of the slice: x: 4, y: 4, z: 8, core: 2. Of those that a mesh axis runs over, the one named last changes fastest.
Arguments:
- multipliers: float32 [256, 4, 128, 128], P(('wide', 'narrow')), may hold values from -6 to 6
- residual_in: float32 [256, 4, 128, 128], P(('wide', 'narrow')), may hold values from -6 to 6
- flexibility: float32 [256, 1024, 1024], P(('wide', 'narrow')), may hold values from -2 to 2, as said below
- stiffness: float32 [256, 1024, 1024], P(('wide', 'narrow')), may hold values from -2 to 2, as said below
- body_modes: float32 [256, 6, 1024], P(('wide', 'narrow')), may hold values from -0.8 to 0.8
- mode_counts: int32 [256], P(('wide', 'narrow')), may hold values from 0 to 6
- iface_index: int32 [256, 1024], P(('wide', 'narrow')), may hold values from 0 to 1023, each once within a row
- coarse_inv: float32 [1536, 1536], P('narrow'), may hold values from -2 to 2, as said below
Outputs:
- multipliers_out: float32 [256, 4, 128, 128], P(('wide', 'narrow'))
- residual_out: float32 [256, 4, 128, 128], P(('wide', 'narrow'))
The draws below stay inside these ranges and needn't reach their ends.
Inputs may be any that keep to these rules, and one draw needn't show every extreme that they name: `iface_index`: each row is a permutation of the local interface unknowns. `flexibility`: symmetric positive definite, diagonal 1 to 2, off-diagonal at most about 0.1. `stiffness`: symmetric positive definite, diagonal 1 to 2, off-diagonal at most about 0.1. `coarse_inv`: symmetric positive definite, diagonal 1 to 2, off-diagonal at most about 0.1.
All inputs are finite; a program needn't handle non-finite values.
Results may differ from the reference program's by a relative error of at most 0.0003.
Values sent between devices are 32-bit elements; how exact they have to be, the bound alone decides.
No kernel may reach another device: no remote copies, remote signals or barrier semaphores. Data moves between devices by JAX's collectives and lax.ppermute only.
A program may use at most 64 MiB of HBM per device.

```python
import jax
import jax.numpy as jnp
from jax import lax

SLOT = 128
IFACE = 1024
MODES = 6
LOADS = 128
ITERS = 2
GRID_A = 32
GRID_B = 8
NSUB = 256
COARSE = 1536


def assemble_operator(key, noise, scale, lowest, highest, count, order):
    diagonal = jax.random.uniform(key, (count, order), jnp.float32, lowest, highest)
    rows = jnp.arange(order)[:, None]
    columns = jnp.arange(order)[None, :]
    mirrored = scale * (noise + jnp.swapaxes(noise, -1, -2))
    return jnp.where(rows == columns, diagonal[:, :, None], mirrored)


def draw_flexibility(key, part):
    key = jax.random.fold_in(key, 11)
    first, second = jax.random.split(key)
    noise = jnp.clip(jax.random.normal(second, (NSUB, IFACE, IFACE), jnp.float32), -5.0, 5.0)
    return assemble_operator(first, noise, 0.25 / IFACE ** 0.5, 1.0, 2.0, NSUB, IFACE)


def draw_stiffness(key, part):
    key = jax.random.fold_in(key, 23)
    first, second = jax.random.split(key)
    noise = jnp.clip(jax.random.normal(second, (NSUB, IFACE, IFACE), jnp.float32), -5.0, 5.0)
    return assemble_operator(first, noise, 0.25 / IFACE ** 0.5, 1.0, 2.0, NSUB, IFACE)


def draw_coarse_inv(key, part):
    key = jax.random.fold_in(key, 37)
    first, second = jax.random.split(key)
    noise = jnp.clip(jax.random.normal(second, (COARSE, COARSE), jnp.float32), -5.0, 5.0)
    diagonal = jax.random.uniform(first, (COARSE,), jnp.float32, 1.0, 2.0)
    rows = jnp.arange(COARSE)[:, None]
    columns = jnp.arange(COARSE)[None, :]
    mirrored = 0.25 / COARSE ** 0.5 * (noise + noise.T)
    return jnp.where(rows == columns, diagonal[:, None], mirrored)


def with_ends(result, stream_key, smallest, top_value):
    index_at = [jax.random.randint(jax.random.fold_in(stream_key, axis), (), 0, length) for axis, length in enumerate(result.shape)]
    longest = result.shape.index(max(result.shape))
    beside = index_at[:longest] + [(index_at[longest] + 1) % result.shape[longest]] + index_at[longest + 1:]
    return result.at[tuple(index_at)].set(smallest).at[tuple(beside)].set(top_value)


def steps_of(key, shape, shards, smallest, largest):
    gain, own = 1.0, jax.random.fold_in(key, 6)
    for axis_at, blocks in shards:
        steps = jnp.exp(jax.random.uniform(jax.random.fold_in(own, axis_at), (blocks,), jnp.float32, smallest / len(shards), largest / len(shards)))
        gain = gain * jnp.repeat(steps, shape[axis_at] // blocks).reshape([-1 if axis == axis_at else 1 for axis in range(len(shape))])
    return gain


def bell_draw(rng, shape, scale, bound, shards=(), held_as=jnp.bfloat16):
    factor_of = steps_of(rng, shape, shards, -0.22, 0.18) if shards else 1.0
    entries = jax.random.normal(rng, shape, jnp.float32) * scale * factor_of
    return jnp.minimum(jnp.maximum(entries, -bound), bound).astype(held_as)


def setup_inputs(seed: int = 0) -> dict:
    splits = jax.random.split(jax.random.key(seed), 9)
    return {
        "multipliers": bell_draw(splits[0], (NSUB, 4, SLOT, LOADS), 1.0, 6.0, ((0, 256),), jnp.float32),
        "residual_in": bell_draw(splits[1], (NSUB, 4, SLOT, LOADS), 1.0, 6.0, ((0, 256),), jnp.float32),
        "flexibility": draw_flexibility(jax.random.fold_in(splits[8], 71), 0),
        "stiffness": draw_stiffness(jax.random.fold_in(splits[8], 71), 0),
        "body_modes": bell_draw(splits[4], (NSUB, MODES, IFACE), 0.1, 0.8, ((0, 256),), jnp.float32),
        "mode_counts": with_ends(jax.random.randint(splits[5], (NSUB,), 0, MODES + 1), jax.random.fold_in(splits[5], 1), 0, MODES).astype(jnp.int32),
        "iface_index": jax.vmap(lambda own: jax.random.permutation(own, IFACE))(jax.random.split(splits[6], NSUB)).reshape((NSUB, IFACE)).astype(jnp.int32),
        "coarse_inv": draw_coarse_inv(jax.random.fold_in(splits[8], 71), 0),
    }


def grid_shift(values, step_a, step_b):
    padded = jnp.pad(values, ((1, 1), (1, 1)) + ((0, 0),) * (values.ndim - 2))
    return padded[1 - step_a:1 - step_a + GRID_A, 1 - step_b:1 - step_b + GRID_B]


def valid_slots():
    pos_a = jnp.arange(GRID_A)[:, None]
    pos_b = jnp.arange(GRID_B)[None, :]
    has_a = pos_a < GRID_A - 1
    has_up = pos_b < GRID_B - 1
    has_down = pos_b > 0
    slots = [has_a & (pos_b >= 0), has_up & (pos_a >= 0), has_a & has_up, has_a & has_down]
    return jnp.stack(slots, axis=-1).astype(jnp.float32)


STEPS = ((1, 0), (0, 1), (1, 1), (1, -1))


def spread_slots(values, iface_index):
    grid = values.reshape(GRID_A, GRID_B, 4, SLOT, LOADS)
    moved = [grid_shift(grid[:, :, k], STEPS[k][0], STEPS[k][1]) for k in range(4)]
    slots = jnp.concatenate([grid, -jnp.stack(moved, axis=2)], axis=2)
    slots = slots.reshape(NSUB, IFACE, LOADS)
    local = jnp.zeros((NSUB, IFACE, LOADS), jnp.float32)
    return local.at[jnp.arange(NSUB)[:, None], iface_index].set(slots)


def collect_jumps(local, iface_index, valid):
    picked = jnp.take_along_axis(local, iface_index[:, :, None], axis=1)
    grid = picked.reshape(GRID_A, GRID_B, 8, SLOT, LOADS)
    jumps = [grid[:, :, k] - grid_shift(grid[:, :, 4 + k], -STEPS[k][0], -STEPS[k][1]) for k in range(4)]
    jumps = jnp.stack(jumps, axis=2) * valid[:, :, :, None, None]
    return jumps.reshape(NSUB, 4, SLOT, LOADS)


def reference(multipliers, residual_in, flexibility, stiffness, body_modes, mode_counts, iface_index, coarse_inv):
    high = lax.Precision.HIGHEST
    valid = valid_slots()
    flat_valid = valid.reshape(NSUB, 4)[:, :, None, None]
    keep = (jnp.arange(MODES)[None, :] < mode_counts[:, None]).astype(jnp.float32)
    masked_modes = body_modes * keep[:, :, None]

    def project(values):
        local = spread_slots(values, iface_index)
        coarse = jnp.einsum("smi,sir->smr", masked_modes, local, precision=high).reshape(COARSE, LOADS)
        solved = jnp.dot(coarse_inv, coarse, precision=high).reshape(NSUB, MODES, LOADS)
        back = jnp.einsum("smi,smr->sir", masked_modes, solved, precision=high)
        return values - collect_jumps(back, iface_index, valid)

    def operate(matrices, values):
        local = spread_slots(values, iface_index)
        product = jnp.einsum("sij,sjr->sir", matrices, local, precision=high)
        return collect_jumps(product, iface_index, valid)

    def inner(first, second):
        return jnp.sum(first * second, axis=(0, 1, 2))

    lam = multipliers * flat_valid
    resid = residual_in * flat_valid
    search = jnp.zeros_like(lam)
    previous = jnp.ones((LOADS,), jnp.float32)
    for iteration in range(ITERS):
        projected = project(resid)
        precond = operate(stiffness, projected)
        curvature = inner(projected, precond)
        along = project(precond)
        if iteration == 0:
            search = along
        else:
            search = along + (curvature / previous) * search
        image = operate(flexibility, search)
        energy = inner(search, image)
        step_size = curvature / energy
        lam = lam + step_size * search
        resid = resid - step_size * image
        previous = curvature
    return lam, resid
```

```python
import jax
import jax.numpy as jnp
import numpy as np
from jax import lax
from jax.experimental import pallas as pl
from jax.experimental.pallas import tpu as pltpu
from jax.sharding import PartitionSpec as P

GRID_A, GRID_B = 32, 8
SLOT, IFACE, MODES, LOADS = 128, 1024, 6, 128
F32, BF16 = jnp.float32, jnp.bfloat16
HIGH = lax.Precision.HIGHEST

STEP = ((1, 0), (0, 1), (1, 1), (1, -1), (-1, 0), (0, -1), (-1, -1), (-1, 1))
ORDER = (1, 2, 7, 5, 3, 6, 0, 4)
AT = {q: p for p, q in enumerate(ORDER)}
PART = 56


def shift(block, axis, distance):
    size = lax.axis_size(axis)
    return lax.ppermute(block, axis, [(i, (i + distance) % size) for i in range(size)])


def exchange(block, axis):
    return lax.all_to_all(block, axis, 0, 0, tiled=True)


def call(body, outs, *args, scratch=(), smem=(), cost=None):
    specs = [
        pl.BlockSpec(memory_space=pltpu.SMEM if i in smem else pltpu.VMEM) for i in range(len(args))
    ]
    return pl.pallas_call(
        body,
        out_shape=[jax.ShapeDtypeStruct(s, d) for s, d in outs],
        in_specs=specs,
        out_specs=[pl.BlockSpec(memory_space=pltpu.VMEM)] * len(outs),
        scratch_shapes=list(scratch),
        compiler_params=pltpu.CompilerParams(vmem_limit_bytes=40 * 1024 * 1024),
        cost_estimate=None
        if cost is None
        else pl.CostEstimate(flops=cost, bytes_accessed=1 << 20, transcendentals=0),
    )(*args)


def halves(x):
    top = x.astype(BF16)
    return top, (x - top.astype(F32)).astype(BF16)


def thirds(x):
    top, rest = x.astype(BF16), None
    rest = x - top.astype(F32)
    mid = rest.astype(BF16)
    return top, mid, (rest - mid.astype(F32)).astype(BF16)


def mm(a, b):
    return jnp.dot(a, b, preferred_element_type=F32)


def mm_nt(a, b):
    return lax.dot_general(a, b, (((1,), (1,)), ((), ())), preferred_element_type=F32)


def fold(x):
    return x[:, :LOADS] + x[:, LOADS:]


def valid_of(place, q):
    a, b = place[0] + STEP[q][0], place[1] + STEP[q][1]
    return ((a >= 0) & (a < GRID_A) & (b >= 0) & (b < GRID_B)).astype(F32)


def rows(p, count=1):
    return slice(p * SLOT, (p + count) * SLOT)


def prepare_kernel(place, index, modes, matrix, pick, put, mode_slots, top, low):
    values = index[...].astype(F32)
    columns = jnp.transpose(jnp.concatenate([values, jnp.zeros((SLOT - 8, SLOT), F32)], axis=0))
    down = lax.broadcasted_iota(jnp.int32, (IFACE, SLOT), 0).astype(F32)
    across = lax.broadcasted_iota(jnp.int32, (SLOT, IFACE), 1).astype(F32)
    for p, q in enumerate(ORDER):
        pick[:, rows(p)] = (down == values[q : q + 1, :]).astype(F32).astype(BF16)
        put[rows(p), :] = (across == columns[:, q : q + 1]).astype(F32).astype(BF16)
    a, b, c = thirds(modes[...])
    stack = jnp.concatenate([a, b, c, jnp.zeros((8, IFACE), BF16)], axis=0)
    for p, q in enumerate(ORDER):
        part = mm(stack, pick[:, rows(p)])
        mode_slots[:, rows(p)] = (part[0:8] + part[8:16] + part[16:24]) * valid_of(place, q)
    split_into(matrix, top, low)


def split_into(matrix, top, low):
    for p in range(8):
        t, l = halves(matrix[0, rows(p), :])
        top[rows(p), :] = t
        low[rows(p), :] = l


def split_kernel(matrix, top, low):
    split_into(matrix, top, low)


def window_kernel(place, inverse, reorder, out):
    first = jnp.clip(place[0] - 1, 0, GRID_A - 3) * (GRID_B * MODES)
    width = GRID_A * GRID_B * MODES
    down = lax.broadcasted_iota(jnp.int32, (width, 256), 0)
    across = lax.broadcasted_iota(jnp.int32, (width, 256), 1)
    choose = (down == across + first).astype(F32).astype(BF16)
    parts = mm(jnp.concatenate(thirds(inverse[...]), axis=0), choose).astype(BF16)
    wide = jnp.concatenate([parts[0:192], parts[192:384], parts[384:576]], axis=1)
    wide = mm(reorder[...], wide)
    out[...] = wide[:, :256] + wide[:, 256:512] + wide[:, 512:]


def coarse_kernel(target, piece, out):
    across = lax.broadcasted_iota(jnp.int32, (8 * PART, 256), 1)
    goal = target[...]
    choose = (across == goal).astype(F32).astype(BF16)
    parts = mm_nt(choose, jnp.concatenate(thirds(piece[...]), axis=0))
    dots = ((goal == -2) & (across % 8 == 6)).astype(F32)
    out[...] = parts[:, :256] + parts[:, 256:512] + parts[:, 512:] + dots


def first_pass_kernel(resid, from_lower, from_upper, mode_slots, ahead, back):
    ahead[0:128] = resid[0, 0]
    ahead[128:256] = from_lower[128:256]
    ahead[256:384] = from_upper[0:128]
    for i, q in enumerate((0, 2, 3)):
        ahead[384 + 8 * i : 392 + 8 * i] = mode_slots[:, rows(AT[q])]
    for i, q in enumerate((4, 6, 7)):
        back[8 * i : 8 * i + 8] = mode_slots[:, rows(AT[q])]


def first_terms_kernel(place, resid, from_lower, from_west, mode_slots, spread, terms):
    own = {q: resid[0, q] for q in range(4)}
    own[5] = -from_lower[0:128]
    own[4] = -from_west[0:128]
    own[6] = -from_west[128:256]
    own[7] = -from_west[256:384]
    total = jnp.zeros((16, 2 * LOADS), F32)
    for p, q in enumerate(ORDER):
        value = own[q] * valid_of(place, q)
        spread[rows(p), :] = value
        modes = jnp.concatenate(halves(mode_slots[:, rows(p)]), axis=0)
        total += mm(modes, jnp.concatenate(halves(value), axis=1))
    total = fold(total)
    total = total[:8] + total[8:]
    for w in range(GRID_A):
        terms[8 * w : 8 * w + 8] = total


def second_pass_kernel(mode_slots, from_west, from_east, up, down):
    up[0:8] = mode_slots[:, rows(AT[1])]
    up[8:16] = from_east[16:24]
    up[16:24] = from_west[392:400]
    down[0:8] = mode_slots[:, rows(AT[5])]
    down[8:16] = from_east[8:16]
    down[16:24] = from_west[400:408]


def modes_kernel(
    place, mode_slots, from_west, from_east, from_lower, from_upper, squeeze, back_top, back_low, gather
):
    has_east = (place[0] < GRID_A - 1).astype(F32)
    has_west = (place[0] > 0).astype(F32)
    west = {q: from_west[384 + 8 * i : 392 + 8 * i] for i, q in enumerate((0, 2, 3))}
    east = {q: from_east[8 * i : 8 * i + 8] for i, q in enumerate((4, 6, 7))}
    facing = {
        0: east[4],
        4: west[0],
        1: from_upper[0:8],
        2: from_upper[8:16],
        7: from_upper[16:24],
        5: from_lower[0:8],
        3: from_lower[8:16],
        6: from_lower[16:24],
    }
    nothing = jnp.zeros((8, SLOT), F32)
    columns = []
    for p, q in enumerate(ORDER):
        blocks = [nothing] * 16
        blocks[4] = mode_slots[:, rows(p)]
        blocks[(STEP[q][0] + 1) * 3 + STEP[q][1] + 1] = -facing[q] * valid_of(place, q)
        columns.append(jnp.transpose(jnp.concatenate(blocks, axis=0)))
    tall = jnp.concatenate(columns, axis=0)
    parts = [mm(t, squeeze[...]) for t in thirds(tall)]
    t, l = halves(parts[0] + parts[1] + parts[2])
    back_top[...] = t[:, :64]
    back_low[...] = l[:, :64]

    here, plus, minus = [nothing] * 14, [nothing] * 14, [nothing] * 14
    for p in range(8):
        here[p] = mode_slots[:, rows(p)]
    here[8] = -mode_slots[:, rows(AT[5])]
    here[11] = -mode_slots[:, rows(AT[1])]
    plus[6], plus[9], plus[12] = (-east[q] * has_east for q in (4, 6, 7))
    minus[7], minus[13], minus[10] = (-west[q] * has_west for q in (0, 2, 3))
    for j in range(14):
        gather[:, rows(j)] = jnp.concatenate(
            halves(jnp.concatenate([here[j], plus[j], minus[j]], axis=0)), axis=0
        )


def pass_on(own_line, from_lower, from_upper, ahead, back):
    ahead[0:128] = own_line[0:128]
    ahead[128:256] = from_lower[128:256]
    ahead[256:384] = from_upper[128:256]
    back[0:128] = own_line[128:256]
    back[128:256] = from_upper[256:384]
    back[256:384] = from_lower[256:384]


def terms_kernel(up, down, own_line, from_lower, from_upper, gather, dots, ahead, back, terms):
    pass_on(own_line, from_lower, from_upper, ahead, back)
    total = jnp.zeros((48, 2 * LOADS), F32)
    at = 0
    for piece in (up, down, own_line, from_lower, from_upper):
        size = piece.shape[0]
        total += mm(gather[:, at : at + size], jnp.concatenate(halves(piece[...]), axis=1))
        at += size
    total = fold(total)
    total = total[:24] + total[24:]
    total = jnp.concatenate([total[:8] + dots[...], total[8:]], axis=0)
    for w in range(GRID_A):
        terms[24 * w : 24 * w + 24] = total


def pass_kernel(own_line, from_lower, from_upper, ahead, back):
    pass_on(own_line, from_lower, from_upper, ahead, back)


def solve_first_kernel(terms, inverse, out):
    out[...] = jnp.dot(inverse[...], terms[...], precision=HIGH, preferred_element_type=F32)


def solve_kernel(terms, inverse, out):
    parts = []
    for w in range(GRID_A):
        e = terms[24 * w : 24 * w + 8]
        if w > 0:
            e = e + terms[24 * w - 16 : 24 * w - 8]
        if w < GRID_A - 1:
            e = e + terms[24 * w + 40 : 24 * w + 48]
        parts.append(e)
    terms = jnp.concatenate(parts, axis=0)
    out[...] = jnp.dot(inverse[...], terms, precision=HIGH, preferred_element_type=F32)


def jump(place, pieces, p):
    up, down, own_line, from_lower, from_upper, from_west, from_east = pieces
    q = ORDER[p]
    own = (up, down, own_line)[p // 3][rows(p % 3), :]
    source, i = {
        1: (from_upper, 0),
        2: (from_east, 1),
        7: (from_west, 2),
        5: (from_lower, 0),
        3: (from_east, 2),
        6: (from_west, 1),
        0: (from_east, 0),
        4: (from_west, 0),
    }[q]
    return (own - source[rows(i), :]) * valid_of(place, q)


def apply_kernel(kind, *refs):
    n_pieces = 1 if kind == "first" else 7
    place, shares, back_top, back_low, pick, put, top, low = refs[:8]
    pieces = refs[8 : 8 + n_pieces]
    rest = refs[8 + n_pieces :]
    old = None
    if kind in ("residual", "search"):
        old, past = rest[:2]
        rest = rest[2:]
    up, down, own_line, field, total, dots = rest[:6]
    rest = rest[6:]
    jumps = None
    if kind == "residual":
        jumps = rest[0]
        rest = rest[1:]
    left, right = rest

    y = shares[0:PART]
    for n in range(1, GRID_B):
        y = y + shares[PART * n : PART * n + PART]
    inner = y[54:55]
    total[...] = jnp.broadcast_to(inner, (8, LOADS))
    yt, yl = halves(jnp.concatenate([y, jnp.zeros((64 - PART, LOADS), F32)], axis=0))
    both = jnp.concatenate([yt, yl], axis=1)
    if kind == "residual":
        factor = past[0:1] / inner
    if kind == "search":
        factor = inner / past[0:1]

    for c in range(4):
        block = slice(256 * c, 256 * c + 256)
        if kind == "first":
            z = pieces[0][block, :]
        else:
            z = jnp.concatenate([jump(place, pieces, 2 * c), jump(place, pieces, 2 * c + 1)], axis=0)
        if kind == "residual":
            jumps[block, :] = z
        f = z - (fold(mm(back_top[block, :], both)) + mm(back_low[block, :], yt))
        if kind == "residual":
            f = old[block, :] - factor * f
        if kind == "search":
            f = f + factor * old[block, :]
        field[block, :] = f
        left[block, :] = jnp.concatenate(halves(f), axis=1)
    for c in range(4):
        block = slice(256 * c, 256 * c + 256)
        right[block, :] = mm(pick[block, :], left[...]).astype(BF16)
    for c in range(4):
        block = slice(256 * c, 256 * c + 256)
        u = fold(mm(top[block, :], right[...])) + mm(low[block, :], right[:, :LOADS])
        left[block, :] = jnp.concatenate(halves(u), axis=1)
    inner = jnp.zeros((1, LOADS), F32)
    for c in range(4):
        block = slice(256 * c, 256 * c + 256)
        u = fold(mm(put[block, :], left[...]))
        inner = inner + jnp.sum(u * field[block, :], axis=0, keepdims=True)
        for h in range(2):
            p = 2 * c + h
            (up, down, own_line)[p // 3][rows(p % 3), :] = u[rows(h)]
    row = lax.broadcasted_iota(jnp.int32, (8, LOADS), 0)
    dots[...] = jnp.where(row == 6, inner, 0.0)


def last_dots_kernel(gathered, out):
    total = gathered[0:8]
    for w in range(1, GRID_A):
        total = total + gathered[8 * w : 8 * w + 8]
    for n in range(GRID_B):
        out[8 * n : 8 * n + 8] = total


def finish_kernel(
    place, shares, *refs
):
    pieces = refs[:7]
    lam, resid, search, search_2, jumps, gamma, delta, gamma_2, lam_out, resid_out = refs[7:]
    energy = shares[0:8]
    for n in range(1, GRID_B):
        energy = energy + shares[8 * n : 8 * n + 8]
    one = gamma[0:1] / delta[0:1]
    two = gamma_2[0:1] / energy[6:7]
    for q in range(4):
        p = AT[q]
        v = valid_of(place, q)
        lam_out[0, q] = lam[0, q] * v + one * search[rows(p), :] + two * search_2[rows(p), :]
        resid_out[0, q] = resid[0, q] * v - one * jumps[rows(p), :] - two * jump(place, pieces, p)


def reorder_rows():
    out = np.zeros((256, 192), np.float32)
    for b in range(8):
        for a in range(4):
            for m in range(MODES):
                out[b * 32 + a * 8 + m, (a * 8 + b) * MODES + m] = 1
    return out


def squeeze_rows():
    out = np.zeros((128, 128), np.float32)
    for g in range(9):
        for m in range(MODES):
            out[g * 8 + m, g * MODES + m] = 1
    return out


def target_tables():
    da = np.full((8 * PART, 1), 1000, np.int32)
    rest = np.full((8 * PART, 1), -1, np.int32)
    for n in range(8):
        for g in range(9):
            for m in range(MODES):
                b = n + g % 3 - 1
                if 0 <= b < GRID_B:
                    da[n * PART + g * MODES + m] = g // 3 - 1
                    rest[n * PART + g * MODES + m] = b * MODES + m
        rest[n * PART + 54] = -2
    return da, rest


def per_device(
    multipliers,
    residual_in,
    flexibility,
    stiffness,
    body_modes,
    mode_counts,
    iface_index,
    coarse_inv,
):
    wide_pos = lax.axis_index("wide")
    place = jnp.stack([wide_pos, lax.axis_index("narrow")]).astype(jnp.int32)
    square = ((IFACE, IFACE), BF16)
    field = ((IFACE, LOADS), F32)
    three = ((3 * SLOT, LOADS), F32)
    two = ((2 * SLOT, LOADS), F32)
    few = ((8, LOADS), F32)

    from_lower = shift(residual_in[0, 1:3].reshape(2 * SLOT, LOADS), "narrow", 1)
    from_upper = shift(residual_in[0, 3], "narrow", -1)
    keep = (jnp.arange(MODES) < mode_counts[0]).astype(F32)
    modes = jnp.pad(body_modes[0] * keep[:, None], ((0, 2), (0, 0)))
    pick, put, mode_slots, stiff_top, stiff_low = call(
        prepare_kernel,
        [square, square, ((8, IFACE), F32), square, square],
        place,
        iface_index.reshape(8, SLOT),
        modes,
        stiffness,
        smem=(0,),
    )
    window = call(
        window_kernel,
        [((256, 256), F32)],
        place,
        coarse_inv,
        jnp.asarray(reorder_rows(), BF16),
        smem=(0,),
    )[0]
    ahead, back = call(
        first_pass_kernel,
        [((408, LOADS), F32), ((24, LOADS), F32)],
        residual_in,
        from_lower,
        from_upper,
        mode_slots,
    )
    from_west = shift(ahead, "wide", 1)
    from_east = shift(back, "wide", -1)
    piece = exchange(window, "narrow")
    da, rest = target_tables()
    first = jnp.clip(wide_pos - 1, 0, GRID_A - 3)
    row = wide_pos + da
    target = jnp.where((row >= 0) & (row < GRID_A), (row - first) * (GRID_B * MODES) + rest, jnp.minimum(rest, -1))
    inverse = call(coarse_kernel, [((8 * PART, 256), F32)], target, piece)[0]
    spread, terms = call(
        first_terms_kernel,
        [field, ((GRID_A * 8, LOADS), F32)],
        place,
        residual_in,
        from_lower,
        from_west,
        mode_slots,
        smem=(0,),
    )
    up, down = call(second_pass_kernel, [((24, LOADS), F32)] * 2, mode_slots, from_west, from_east)
    modes_lower = shift(up, "narrow", 1)
    modes_upper = shift(down, "narrow", -1)
    flex_top, flex_low = call(split_kernel, [square, square], flexibility)
    terms = exchange(terms, "wide")
    shares = exchange(
        call(solve_first_kernel, [((8 * PART, LOADS), F32)], terms, inverse)[0], "narrow"
    )
    back_top, back_low, gather = call(
        modes_kernel,
        [((IFACE, 64), BF16), ((IFACE, 64), BF16), ((48, 14 * SLOT), BF16)],
        place,
        mode_slots,
        from_west,
        from_east,
        modes_lower,
        modes_upper,
        jnp.asarray(squeeze_rows(), BF16),
        smem=(0,),
    )

    def apply(kind, shares, matrix, pieces, *old):
        outs = [three, three, two, field, few, few] + ([field] if kind == "residual" else [])

        def body(*refs):
            apply_kernel(kind, *refs)

        return call(
            body,
            outs,
            place,
            shares,
            back_top,
            back_low,
            pick,
            put,
            *matrix,
            *pieces,
            *old,
            smem=(0,),
            scratch=[pltpu.VMEM((IFACE, 2 * LOADS), BF16)] * 2,
        )

    def across(up, down):
        return shift(up, "narrow", 1), shift(down, "narrow", -1)

    def coarse(up, down, own_line, dots):
        from_lower, from_upper = across(up, down)
        ahead, back, terms = call(
            terms_kernel,
            [three, three, ((GRID_A * 24, LOADS), F32)],
            up,
            down,
            own_line,
            from_lower,
            from_upper,
            gather,
            dots,
        )
        from_west = shift(ahead, "wide", 1)
        from_east = shift(back, "wide", -1)
        terms = exchange(terms, "wide")
        shares = exchange(
            call(solve_kernel, [((8 * PART, LOADS), F32)], terms, inverse)[0], "narrow"
        )
        return shares, (up, down, own_line, from_lower, from_upper, from_west, from_east)

    stiff, flex = (stiff_top, stiff_low), (flex_top, flex_low)
    up, down, own_line, proj, _, dots = apply("first", shares, stiff, (spread,))
    shares, pieces = coarse(up, down, own_line, dots)
    up, down, own_line, search, gamma, dots = apply("plain", shares, flex, pieces)
    shares, pieces = coarse(up, down, own_line, dots)
    up, down, own_line, _, delta, dots, image = apply("residual", shares, stiff, pieces, proj, gamma)
    shares, pieces = coarse(up, down, own_line, dots)
    up, down, own_line, search_2, gamma_2, dots = apply("search", shares, flex, pieces, search, gamma)

    from_lower, from_upper = across(up, down)
    ahead, back = call(pass_kernel, [three, three], own_line, from_lower, from_upper)
    from_west = shift(ahead, "wide", 1)
    from_east = shift(back, "wide", -1)
    gathered = exchange(jnp.tile(dots, (GRID_A, 1)), "wide")
    shares = exchange(call(last_dots_kernel, [((64, LOADS), F32)], gathered)[0], "narrow")
    out = ((1, 4, SLOT, LOADS), F32)
    return tuple(
        call(
            finish_kernel,
            [out, out],
            place,
            shares,
            up,
            down,
            own_line,
            from_lower,
            from_upper,
            from_west,
            from_east,
            multipliers,
            residual_in,
            search,
            search_2,
            image,
            gamma,
            delta,
            gamma_2,
            smem=(0,),
        )
    )


def solution(mesh):
    both = ("wide", "narrow")
    in_specs = (
        P(both, None, None, None),
        P(both, None, None, None),
        P(both, None, None),
        P(both, None, None),
        P(both, None, None),
        P(both),
        P(both, None),
        P("narrow", None),
    )
    out_specs = (P(both, None, None, None), P(both, None, None, None))
    return jax.shard_map(
        per_device, mesh=mesh, in_specs=in_specs, out_specs=out_specs, check_vma=False
    )
```

```python
import jax
import jax.numpy as jnp
from jax import lax
from jax.experimental import pallas as pl
from jax.experimental.pallas import tpu as pltpu
from jax.sharding import PartitionSpec as P

GRID_A, GRID_B = 32, 8
SLOT, IFACE, MODES, LOADS = 128, 1024, 6, 128
F32, BF16 = jnp.float32, jnp.bfloat16
HIGH = lax.Precision.HIGHEST

STEP = ((1, 0), (0, 1), (1, 1), (1, -1), (-1, 0), (0, -1), (-1, -1), (-1, 1))
ORDER = (0, 2, 3, 4, 6, 7, 1, 5)
AT = {q: p for p, q in enumerate(ORDER)}
PART = 80
CHIPS = GRID_B // 2


def shift(block, axis, distance):
    size = lax.axis_size(axis)
    return lax.ppermute(block, axis, [(i, (i + distance) % size) for i in range(size)])


def exchange(block, axis):
    return lax.all_to_all(block, axis, 0, 0, tiled=True)


def call(body, outs, *args, scratch=(), smem=(), far=(), bytes_moved=None):
    specs = [
        pl.BlockSpec(
            memory_space=pltpu.SMEM if i in smem else pltpu.HBM if i in far else pltpu.VMEM
        )
        for i in range(len(args))
    ]
    return pl.pallas_call(
        body,
        out_shape=[jax.ShapeDtypeStruct(s, d) for s, d in outs],
        in_specs=specs,
        out_specs=[pl.BlockSpec(memory_space=pltpu.VMEM)] * len(outs),
        scratch_shapes=list(scratch),
        compiler_params=pltpu.CompilerParams(vmem_limit_bytes=16 * 1024 * 1024),
        cost_estimate=None
        if bytes_moved is None
        else pl.CostEstimate(flops=0, bytes_accessed=bytes_moved, transcendentals=0),
    )(*args)


def halves(x):
    top = x.astype(BF16)
    return top, (x - top.astype(F32)).astype(BF16)


def thirds(x):
    top, rest = x.astype(BF16), None
    rest = x - top.astype(F32)
    mid = rest.astype(BF16)
    return top, mid, (rest - mid.astype(F32)).astype(BF16)


def mm(a, b):
    return jnp.dot(a, b, preferred_element_type=F32)


def mm_nt(a, b):
    return lax.dot_general(a, b, (((1,), (1,)), ((), ())), preferred_element_type=F32)


def fold(x):
    return x[:, :LOADS] + x[:, LOADS:]


def valid_of(place, q):
    a, b = place[0] + STEP[q][0], place[1] + STEP[q][1]
    return ((a >= 0) & (a < GRID_A) & (b >= 0) & (b < GRID_B)).astype(F32)


def rows(p, count=1):
    return slice(p * SLOT, (p + count) * SLOT)


def columns_of(index):
    values = index[...].astype(F32)
    return jnp.transpose(jnp.concatenate([values, jnp.zeros((SLOT - 8, SLOT), F32)], axis=0))


def iota(shape, axis):
    return lax.broadcasted_iota(jnp.int32, shape, axis)


def one_hot(condition):
    return condition.astype(F32).astype(BF16)


def steps_at(x, *bounds):
    return sum((x >= b).astype(jnp.int32) for b in bounds)


def prepare_kernel(place, counts, index, modes, inverse, mode_slots, ahead, back, window, held, arrived):
    width = GRID_A * GRID_B * MODES
    first = jnp.clip(place[0] - 1, 0, GRID_A - 3) * (GRID_B * MODES)
    start = pl.multiple_of(jnp.minimum(first // 128 * 128, width - 384), 128)
    copy = pltpu.make_async_copy(inverse.at[:, pl.ds(start, 384)], held, arrived)
    copy.start()

    keep = iota((8, SLOT), 0) < counts[0]
    pieces = []
    for j in range(8):
        own = jnp.concatenate([modes[pl.ds(j, MODES, stride=8), :], jnp.zeros((8 - MODES, SLOT), F32)], axis=0)
        a, b, c = thirds(jnp.where(keep, own, 0.0))
        pieces.append(jnp.concatenate([a, b, c, jnp.zeros((8, SLOT), BF16)], axis=0))
    stack = jnp.concatenate(pieces, axis=1)
    values = index[...].astype(F32)
    at = iota((IFACE, SLOT), 0).astype(F32)
    for p, q in enumerate(ORDER):
        part = mm(stack, one_hot(at == values[q : q + 1, :]))
        part = (part[0:8] + part[8:16] + part[16:24]) * valid_of(place, q)
        mode_slots[:, rows(p)] = part
        if p < 6:
            (ahead, back)[p // 3][8 * (p % 3) : 8 * (p % 3) + 8] = part

    copy.wait()
    choose = one_hot(iota((384, 256), 0) == iota((384, 256), 1) + (first - start))
    parts = mm(jnp.concatenate(thirds(held[...]), axis=0), choose).astype(BF16)
    wide = jnp.concatenate([parts[0:192], parts[192:384], parts[384:576]], axis=1)
    r = iota((256, 192), 0)
    source = (((r >> 3) & 3) * GRID_B + (r >> 5)) * MODES + (r & 7)
    wide = mm(one_hot((iota((256, 192), 1) == source) & ((r & 7) < MODES)), wide)
    window[...] = wide[:, :256] + wide[:, 256:512] + wide[:, 512:]


def first_pass_kernel(place, resid, from_west, modes_west, modes_east, mode_slots, piece, up, down, inverse, token):
    up[0:128] = resid[0, 1]
    up[128:256] = from_west[0, 2]
    up[256:264] = mode_slots[:, rows(AT[1])]
    up[264:272] = modes_west[8:16]
    up[272:280] = modes_east[16:24]
    down[0:128] = from_west[0, 3]
    down[128:136] = mode_slots[:, rows(AT[5])]
    down[136:144] = modes_west[16:24]
    down[144:152] = modes_east[8:16]
    token[...] = jnp.zeros((8, LOADS), F32)

    shape = (CHIPS * PART, 256)
    row, across = iota(shape, 0), iota(shape, 1)
    j = steps_at(row, PART, 2 * PART, 3 * PART)
    r = row - PART * j
    d = steps_at(r, 24, 48, 72)
    m = r - 24 * d
    offset = steps_at(m, 6, 12, 18)
    m = m - MODES * offset
    b = 2 * ((place[1] // 2 + j) & (CHIPS - 1)) - 1 + offset
    a = place[0] + d - 1
    goal = (a - jnp.clip(place[0] - 1, 0, GRID_A - 3)) * (GRID_B * MODES) + b * MODES + m
    real = (r < 72) & (b >= 0) & (b < GRID_B) & (a >= 0) & (a < GRID_A)
    parts = mm_nt(one_hot(real & (across == goal)), jnp.concatenate(thirds(piece[...]), axis=0))
    dots = ((r == 72) & ((across & 7) == 6)).astype(F32)
    inverse[...] = parts[:, :256] + parts[:, 256:512] + parts[:, 512:] + dots


def split_kernel(token, matrix, top, low, token_out, held, arrived):
    blocks = [slice(256 * c, 256 * c + 256) for c in range(4)]
    copies = [
        pltpu.make_async_copy(matrix.at[0, block, :], held.at[block, :], arrived.at[c])
        for c, block in enumerate(blocks)
    ]
    for copy in copies:
        copy.start()
    token_out[...] = token[...]
    for copy, block in zip(copies, blocks):
        copy.wait()
        top[block, :], low[block, :] = halves(held[block, :])


def split_first_kernel(token, index, matrix, top, low, pick, put, token_out, held, arrived):
    split_kernel(token, matrix, top, low, token_out, held, arrived)
    values, columns = index[...].astype(F32), columns_of(index)
    down = iota((IFACE, SLOT), 0).astype(F32)
    across = iota((SLOT, IFACE), 1).astype(F32)
    for p, q in enumerate(ORDER):
        pick[:, rows(p)] = one_hot(down == values[q : q + 1, :])
        put[rows(p), :] = one_hot(across == columns[:, q : q + 1])


def first_terms_kernel(
    place, resid, from_west, from_lower, from_upper, modes_west, modes_east, mode_slots, token,
    spread, terms, back_top, back_low, gather,
):
    own = {q: resid[0, q] for q in range(4)}
    own[4] = -from_west[0, 0]
    own[5] = -from_lower[0:128]
    own[6] = -from_lower[128:256]
    own[7] = -from_upper[0:128]
    total = jnp.zeros((16, 2 * LOADS), F32)
    for p, q in enumerate(ORDER):
        value = own[q] * valid_of(place, q)
        spread[rows(p), :] = value
        modes = jnp.concatenate(halves(mode_slots[:, rows(p)]), axis=0)
        gather[:, rows(p)] = modes
        total += mm(modes, jnp.concatenate(halves(value), axis=1))
    put_terms(total, token[...], terms)

    facing = {
        0: modes_east[0:8],
        4: modes_west[0:8],
        1: from_upper[128:136],
        7: from_upper[136:144],
        2: from_upper[144:152],
        5: from_lower[256:264],
        6: from_lower[264:272],
        3: from_lower[272:280],
    }
    nothing = jnp.zeros((8, SLOT), F32)
    columns = []
    for p, q in enumerate(ORDER):
        blocks = [nothing] * 16
        blocks[4] = mode_slots[:, rows(p)]
        blocks[(STEP[q][0] + 1) * 3 + STEP[q][1] + 1] = -facing[q] * valid_of(place, q)
        columns.append(jnp.transpose(jnp.concatenate(blocks, axis=0)))
    tall = jnp.concatenate(columns, axis=0)
    r, to = iota((128, 128), 0), iota((128, 128), 1)
    g, m = r >> 3, r & 7
    d = steps_at(g, 3, 6)
    choose = one_hot((g < 9) & (m < MODES) & (to == d * 24 + (g - 3 * d + place[1] % 2) * MODES + m))
    parts = [mm(t, choose) for t in thirds(tall)]
    back_top[...], back_low[...] = halves(parts[0] + parts[1] + parts[2])


def put_terms(total, dots, terms):
    total = fold(total)
    total = total[:8] + total[8:] + dots
    for w in range(GRID_A):
        terms[8 * w : 8 * w + 8] = total


def pass_kernel(line, from_west, from_east, up, down):
    up[0:128] = line[0:128]
    up[128:256] = from_west[128:256]
    up[256:384] = from_east[256:384]
    down[0:128] = line[128:256]
    down[128:256] = from_west[256:384]
    down[256:384] = from_east[128:256]


def terms_kernel(
    place, ahead, back, line, from_west, from_east, from_lower, from_upper, gather, dots, token, spread, terms
):
    total = jnp.zeros((16, 2 * LOADS), F32)
    for p, q in enumerate(ORDER):
        own = (ahead, back, line)[p // 3][rows(p % 3), :]
        source, i = {
            0: (from_east, 0),
            4: (from_west, 0),
            1: (from_upper, 0),
            7: (from_upper, 1),
            2: (from_upper, 2),
            5: (from_lower, 0),
            6: (from_lower, 1),
            3: (from_lower, 2),
        }[q]
        value = (own - source[rows(i), :]) * valid_of(place, q)
        spread[rows(p), :] = value
        total += mm(gather[:, rows(p)], jnp.concatenate(halves(value), axis=1))
    put_terms(total, dots[...], terms)


def solve_kernel(terms, inverse, *outs):
    out = jnp.dot(inverse[...], terms[...], precision=HIGH, preferred_element_type=F32)
    for j in range(CHIPS):
        outs[j][...] = out[PART * j : PART * j + PART]


def sum_kernel(*refs):
    refs[-1][...] = (refs[0][...] + refs[1][...]) + (refs[2][...] + refs[3][...])


def apply_kernel(kind, *refs):
    place, share, other, back_top, back_low, pick, put, top, low, spread = refs[:10]
    rest = refs[10:]
    old = None
    if kind in ("residual", "search"):
        old, past = rest[:2]
        rest = rest[2:]
    if kind == "residual":
        lam, resid, search = rest[:3]
        rest = rest[3:]
    ahead, back, line, field, total, dots = rest[:6]
    rest = rest[6:]
    if kind == "residual":
        lam_out, resid_out = rest[:2]
        rest = rest[2:]
    left, right = rest

    y = share[...] + other[...]
    inner = y[72:73]
    total[...] = jnp.broadcast_to(inner, (8, LOADS))
    yt, yl = halves(jnp.concatenate([y, jnp.zeros((128 - PART, LOADS), F32)], axis=0))
    both = jnp.concatenate([yt, yl], axis=1)
    if kind == "residual":
        factor = past[0:1] / inner
        for q in range(4):
            p = AT[q]
            v = valid_of(place, q)
            lam_out[rows(q), :] = lam[0, q] * v + factor * search[rows(p), :]
            resid_out[rows(q), :] = resid[0, q] * v - factor * spread[rows(p), :]
    if kind == "search":
        factor = inner / past[0:1]

    blocks = [slice(256 * c, 256 * c + 256) for c in range(4)]
    for block in blocks:
        f = spread[block, :] - (fold(mm(back_top[block, :], both)) + mm(back_low[block, :], yt))
        if kind == "residual":
            f = old[block, :] - factor * f
        if kind == "search":
            f = f + factor * old[block, :]
        field[block, :] = f
        left[block, :] = jnp.concatenate(halves(f), axis=1)
    for block in blocks:
        right[block, :] = mm(pick[block, :], left[...]).astype(BF16)
    for block in blocks:
        u = fold(mm(top[block, :], right[...])) + mm(low[block, :], right[:, :LOADS])
        left[block, :] = jnp.concatenate(halves(u), axis=1)
    inner = jnp.zeros((1, LOADS), F32)
    for c, block in enumerate(blocks):
        u = fold(mm(put[block, :], left[...]))
        inner = inner + jnp.sum(u * field[block, :], axis=0, keepdims=True)
        for h in range(2):
            p = 2 * c + h
            (ahead, back, line)[p // 3][rows(p % 3), :] = u[rows(h)]
    row = iota(dots.shape, 0) & 7
    dots[...] = jnp.where(row == 6, inner, 0.0)


def last_pass_kernel(line, from_east, up, down):
    up[...] = from_east[256:384]
    down[0:128] = line[128:256]
    down[128:256] = from_east[128:256]


def last_dots_kernel(gathered, out):
    total = gathered[0:8]
    for w in range(1, GRID_A):
        total = total + gathered[8 * w : 8 * w + 8]
    for n in range(GRID_B):
        out[8 * n : 8 * n + 8] = total


def finish_kernel(
    place, shares, lam, resid, search, gamma, ahead, line, from_east, from_lower, from_upper, lam_out, resid_out
):
    energy = shares[0:8]
    for n in range(1, GRID_B):
        energy = energy + shares[8 * n : 8 * n + 8]
    step = gamma[0:1] / energy[6:7]
    for q, own, facing in (
        (0, ahead[0:128], from_east[0:128]),
        (1, line[0:128], from_upper[0:128]),
        (2, ahead[128:256], from_upper[128:256]),
        (3, ahead[256:384], from_lower[...]),
    ):
        lam_out[0, q] = lam[rows(q), :] + step * search[rows(AT[q]), :]
        resid_out[0, q] = resid[rows(q), :] - step * (valid_of(place, q) * (own - facing))


def per_device(
    multipliers,
    residual_in,
    flexibility,
    stiffness,
    body_modes,
    mode_counts,
    iface_index,
    coarse_inv,
):
    place = jnp.stack([lax.axis_index("wide"), lax.axis_index("narrow")]).astype(jnp.int32)
    square = ((IFACE, IFACE), BF16)
    field = ((IFACE, LOADS), F32)
    three = ((3 * SLOT, LOADS), F32)
    two = ((2 * SLOT, LOADS), F32)
    one = ((SLOT, LOADS), F32)
    few = ((8, LOADS), F32)
    thin = ((24, LOADS), F32)
    terms_shape = ((GRID_A * 8, LOADS), F32)
    index = iface_index.reshape(8, SLOT)
    stream = [pltpu.VMEM((IFACE, IFACE), F32), pltpu.SemaphoreType.DMA((4,))]

    def solve(terms, inverse):
        terms = exchange(terms, "wide")
        parts = call(solve_kernel, [((PART, LOADS), F32)] * CHIPS, terms, inverse)
        parts = [parts[0]] + [shift(parts[j], "narrow", 2 * j) for j in range(1, CHIPS)]
        share = call(sum_kernel, [((PART, LOADS), F32)], *parts)[0]
        return share, lax.ppermute(share, "narrow", [(i, i ^ 1) for i in range(GRID_B)])

    from_west = shift(residual_in, "wide", 1)
    mode_slots, ahead, back, window = call(
        prepare_kernel,
        [((8, IFACE), F32), thin, thin, ((256, 256), F32)],
        place,
        mode_counts,
        index,
        body_modes.reshape(8 * MODES, SLOT),
        coarse_inv,
        smem=(0, 1),
        far=(4,),
        scratch=[pltpu.VMEM((192, 384), F32), pltpu.SemaphoreType.DMA],
    )
    modes_west = shift(ahead, "wide", 1)
    modes_east = shift(back, "wide", -1)
    piece = exchange(window, "narrow")
    up, down, inverse, token = call(
        first_pass_kernel,
        [((280, LOADS), F32), ((152, LOADS), F32), ((CHIPS * PART, 256), F32), few],
        place,
        residual_in,
        from_west,
        modes_west,
        modes_east,
        mode_slots,
        piece,
        smem=(0,),
    )
    from_lower = shift(up, "narrow", 1)
    from_upper = shift(down, "narrow", -1)
    *stiff, pick, put, token = call(
        split_first_kernel,
        [square] * 4 + [few],
        token,
        index,
        stiffness,
        far=(2,),
        scratch=stream,
        bytes_moved=1 << 23,
    )
    spread, terms, back_top, back_low, gather = call(
        first_terms_kernel,
        [field, terms_shape] + [((IFACE, 128), BF16)] * 2 + [((16, IFACE), BF16)],
        place,
        residual_in,
        from_west,
        from_lower,
        from_upper,
        modes_west,
        modes_east,
        mode_slots,
        token,
        smem=(0,),
    )
    shares = solve(terms, inverse)

    def apply(kind, shares, matrix, spread, *old, last=False):
        outs = [three, three, two, field, few, terms_shape if last else few]
        if kind == "residual":
            outs += [((4 * SLOT, LOADS), F32)] * 2

        def body(*refs):
            apply_kernel(kind, *refs)

        return call(
            body,
            outs,
            place,
            *shares,
            back_top,
            back_low,
            pick,
            put,
            *matrix,
            spread,
            *old,
            smem=(0,),
            scratch=[pltpu.VMEM((IFACE, 2 * LOADS), BF16)] * 2,
        )

    def coarse(ahead, back, line, dots, token):
        from_west = shift(ahead, "wide", 1)
        from_east = shift(back, "wide", -1)
        up, down = call(pass_kernel, [three, three], line, from_west, from_east)
        from_lower = shift(up, "narrow", 1)
        from_upper = shift(down, "narrow", -1)
        spread, terms = call(
            terms_kernel,
            [field, terms_shape],
            place,
            ahead,
            back,
            line,
            from_west,
            from_east,
            from_lower,
            from_upper,
            gather,
            dots,
            token,
            smem=(0,),
        )
        return solve(terms, inverse), spread

    ahead, back, line, proj, _, dots = apply("first", shares, stiff, spread)
    *flex, token = call(
        split_kernel,
        [square, square, few],
        dots,
        flexibility,
        far=(1,),
        scratch=stream,
        bytes_moved=1 << 23,
    )
    shares, spread = coarse(ahead, back, line, dots, token)
    ahead, back, line, search, gamma, dots = apply("plain", shares, flex, spread)
    shares, spread = coarse(ahead, back, line, dots, token)
    ahead, back, line, _, _, dots, lam, resid = apply(
        "residual", shares, stiff, spread, proj, gamma, multipliers, residual_in, search
    )
    shares, spread = coarse(ahead, back, line, dots, token)
    ahead, back, line, search, gamma, dots = apply(
        "search", shares, flex, spread, search, gamma, last=True
    )

    from_east = shift(back, "wide", -1)
    gathered = exchange(dots, "wide")
    up, down = call(last_pass_kernel, [one, two], line, from_east)
    from_lower = shift(up, "narrow", 1)
    from_upper = shift(down, "narrow", -1)
    shares = exchange(call(last_dots_kernel, [((64, LOADS), F32)], gathered)[0], "narrow")
    out = ((1, 4, SLOT, LOADS), F32)
    return tuple(
        call(
            finish_kernel,
            [out, out],
            place,
            shares,
            lam,
            resid,
            search,
            gamma,
            ahead,
            line,
            from_east,
            from_lower,
            from_upper,
            smem=(0,),
        )
    )


def solution(mesh):
    both = ("wide", "narrow")
    in_specs = (
        P(both, None, None, None),
        P(both, None, None, None),
        P(both, None, None),
        P(both, None, None),
        P(both, None, None),
        P(both),
        P(both, None),
        P("narrow", None),
    )
    out_specs = (P(both, None, None, None), P(both, None, None, None))
    return jax.shard_map(
        per_device, mesh=mesh, in_specs=in_specs, out_specs=out_specs, check_vma=False
    )
```

```python
import jax
import jax.numpy as jnp
from jax import lax
from jax.experimental import pallas as pl
from jax.experimental.pallas import tpu as pltpu
from jax.sharding import PartitionSpec as P

GRID_A, GRID_B = 32, 8
SLOT, IFACE, MODES, LOADS = 128, 1024, 6, 128
F32, BF16 = jnp.float32, jnp.bfloat16
HIGH = lax.Precision.HIGHEST

STEP = ((1, 0), (0, 1), (1, 1), (1, -1), (-1, 0), (0, -1), (-1, -1), (-1, 1))
ORDER = (0, 2, 3, 4, 6, 7, 1, 5)
AT = {q: p for p, q in enumerate(ORDER)}
PART = 80
CHIPS = GRID_B // 2


def shift(block, axis, distance):
    size = lax.axis_size(axis)
    return lax.ppermute(block, axis, [(i, (i + distance) % size) for i in range(size)])


def exchange(block, axis, groups=None):
    return lax.all_to_all(block, axis, 0, 0, tiled=True, axis_index_groups=groups)


LINES = [[w * 8 + n for w in range(8 * y, 8 * y + 8) for n in (2 * x, 2 * x + 1)] for y in range(4) for x in range(4)]
PLANES = [[w * 8 + n for w in range(z, 32, 8) for n in range(c, 8, 2)] for z in range(8) for c in range(2)]


def call(body, outs, *args, scratch=(), smem=(), far=(), bytes_moved=None, grant=16):
    specs = [
        pl.BlockSpec(
            memory_space=pltpu.SMEM if i in smem else pltpu.HBM if i in far else pltpu.VMEM
        )
        for i in range(len(args))
    ]
    return pl.pallas_call(
        body,
        out_shape=[jax.ShapeDtypeStruct(s, d) for s, d in outs],
        in_specs=specs,
        out_specs=[pl.BlockSpec(memory_space=pltpu.VMEM)] * len(outs),
        scratch_shapes=list(scratch),
        compiler_params=pltpu.CompilerParams(vmem_limit_bytes=grant * 1024 * 1024),
        cost_estimate=None
        if bytes_moved is None
        else pl.CostEstimate(flops=0, bytes_accessed=bytes_moved, transcendentals=0),
    )(*args)


def halves(x):
    top = x.astype(BF16)
    return top, (x - top.astype(F32)).astype(BF16)


def thirds(x):
    top, rest = x.astype(BF16), None
    rest = x - top.astype(F32)
    mid = rest.astype(BF16)
    return top, mid, (rest - mid.astype(F32)).astype(BF16)


def mm(a, b):
    return jnp.dot(a, b, preferred_element_type=F32)


def mm_nt(a, b):
    return lax.dot_general(a, b, (((1,), (1,)), ((), ())), preferred_element_type=F32)


def fold(x):
    return x[:, :LOADS] + x[:, LOADS:]


def valid_of(place, q):
    a, b = place[0] + STEP[q][0], place[1] + STEP[q][1]
    return ((a >= 0) & (a < GRID_A) & (b >= 0) & (b < GRID_B)).astype(F32)


def rows(p, count=1):
    return slice(p * SLOT, (p + count) * SLOT)


def columns_of(index):
    values = index[...].astype(F32)
    return jnp.transpose(jnp.concatenate([values, jnp.zeros((SLOT - 8, SLOT), F32)], axis=0))


def iota(shape, axis):
    return lax.broadcasted_iota(jnp.int32, shape, axis)


def one_hot(condition):
    return condition.astype(F32).astype(BF16)


def steps_at(x, *bounds):
    return sum((x >= b).astype(jnp.int32) for b in bounds)


def prepare_kernel(place, counts, index, modes, inverse, mode_slots, ahead, back, window, held, arrived):
    width = GRID_A * GRID_B * MODES
    first = jnp.clip(place[0] - 1, 0, GRID_A - 3) * (GRID_B * MODES)
    start = pl.multiple_of(jnp.minimum(first // 128 * 128, width - 384), 128)
    copy = pltpu.make_async_copy(inverse.at[:, pl.ds(start, 384)], held, arrived)
    copy.start()

    keep = iota((8, SLOT), 0) < counts[0]
    pieces = []
    for j in range(8):
        own = jnp.concatenate([modes[pl.ds(j, MODES, stride=8), :], jnp.zeros((8 - MODES, SLOT), F32)], axis=0)
        a, b, c = thirds(jnp.where(keep, own, 0.0))
        pieces.append(jnp.concatenate([a, b, c, jnp.zeros((8, SLOT), BF16)], axis=0))
    stack = jnp.concatenate(pieces, axis=1)
    values = index[...].astype(F32)
    at = iota((IFACE, SLOT), 0).astype(F32)
    for p, q in enumerate(ORDER):
        part = mm(stack, one_hot(at == values[q : q + 1, :]))
        part = (part[0:8] + part[8:16] + part[16:24]) * valid_of(place, q)
        mode_slots[:, rows(p)] = part
        if p < 6:
            (ahead, back)[p // 3][8 * (p % 3) : 8 * (p % 3) + 8] = part

    copy.wait()
    choose = one_hot(iota((384, 256), 0) == iota((384, 256), 1) + (first - start))
    parts = mm(jnp.concatenate(thirds(held[...]), axis=0), choose).astype(BF16)
    wide = jnp.concatenate([parts[0:192], parts[192:384], parts[384:576]], axis=1)
    r = iota((256, 192), 0)
    source = (((r >> 3) & 3) * GRID_B + (r >> 5)) * MODES + (r & 7)
    wide = mm(one_hot((iota((256, 192), 1) == source) & ((r & 7) < MODES)), wide)
    window[...] = wide[:, :256] + wide[:, 256:512] + wide[:, 512:]


def first_pass_kernel(place, resid, from_west, modes_west, modes_east, mode_slots, piece, up, down, inverse, token):
    up[0:128] = resid[0, 1]
    up[128:256] = from_west[0, 2]
    up[256:264] = mode_slots[:, rows(AT[1])]
    up[264:272] = modes_west[8:16]
    up[272:280] = modes_east[16:24]
    down[0:128] = from_west[0, 3]
    down[128:136] = mode_slots[:, rows(AT[5])]
    down[136:144] = modes_west[16:24]
    down[144:152] = modes_east[8:16]
    token[...] = jnp.zeros((8, LOADS), F32)

    shape = (CHIPS * PART, 256)
    row, across = iota(shape, 0), iota(shape, 1)
    j = steps_at(row, PART, 2 * PART, 3 * PART)
    r = row - PART * j
    d = steps_at(r, 24, 48, 72)
    m = r - 24 * d
    offset = steps_at(m, 6, 12, 18)
    m = m - MODES * offset
    b = 2 * ((place[1] // 2 + j) & (CHIPS - 1)) - 1 + offset
    a = place[0] + d - 1
    goal = (a - jnp.clip(place[0] - 1, 0, GRID_A - 3)) * (GRID_B * MODES) + b * MODES + m
    real = (r < 72) & (b >= 0) & (b < GRID_B) & (a >= 0) & (a < GRID_A)
    parts = mm_nt(one_hot(real & (across == goal)), jnp.concatenate(thirds(piece[...]), axis=0))
    dots = ((r == 72) & ((across & 7) == 6)).astype(F32)
    inverse[...] = parts[:, :256] + parts[:, 256:512] + parts[:, 512:] + dots


def split_kernel(token, matrix, top, low, token_out, held, arrived):
    blocks = [slice(256 * c, 256 * c + 256) for c in range(4)]
    copies = [
        pltpu.make_async_copy(matrix.at[0, block, :], held.at[block, :], arrived.at[c])
        for c, block in enumerate(blocks)
    ]
    for copy in copies:
        copy.start()
    token_out[...] = token[...]
    for copy, block in zip(copies, blocks):
        copy.wait()
        top[block, :], low[block, :] = halves(held[block, :])


def split_first_kernel(token, index, matrix, top, low, pick, put, token_out, held, arrived):
    split_kernel(token, matrix, top, low, token_out, held, arrived)
    values, columns = index[...].astype(F32), columns_of(index)
    down = iota((IFACE, SLOT), 0).astype(F32)
    across = iota((SLOT, IFACE), 1).astype(F32)
    for p, q in enumerate(ORDER):
        pick[:, rows(p)] = one_hot(down == values[q : q + 1, :])
        put[rows(p), :] = one_hot(across == columns[:, q : q + 1])


def first_terms_kernel(
    place, resid, from_west, from_lower, from_upper, modes_west, modes_east, mode_slots, token,
    spread, terms, back_top, back_low, gather,
):
    own = {q: resid[0, q] for q in range(4)}
    own[4] = -from_west[0, 0]
    own[5] = -from_lower[0:128]
    own[6] = -from_lower[128:256]
    own[7] = -from_upper[0:128]
    total = jnp.zeros((16, 2 * LOADS), F32)
    for p, q in enumerate(ORDER):
        value = own[q] * valid_of(place, q)
        spread[rows(p), :] = value
        modes = jnp.concatenate(halves(mode_slots[:, rows(p)]), axis=0)
        gather[:, rows(p)] = modes
        total += mm(modes, jnp.concatenate(halves(value), axis=1))
    put_terms(total, token[...], terms)

    facing = {
        0: modes_east[0:8],
        4: modes_west[0:8],
        1: from_upper[128:136],
        7: from_upper[136:144],
        2: from_upper[144:152],
        5: from_lower[256:264],
        6: from_lower[264:272],
        3: from_lower[272:280],
    }
    nothing = jnp.zeros((8, SLOT), F32)
    columns = []
    for p, q in enumerate(ORDER):
        blocks = [nothing] * 16
        blocks[4] = mode_slots[:, rows(p)]
        blocks[(STEP[q][0] + 1) * 3 + STEP[q][1] + 1] = -facing[q] * valid_of(place, q)
        columns.append(jnp.transpose(jnp.concatenate(blocks, axis=0)))
    tall = jnp.concatenate(columns, axis=0)
    r, to = iota((128, 128), 0), iota((128, 128), 1)
    g, m = r >> 3, r & 7
    d = steps_at(g, 3, 6)
    choose = one_hot((g < 9) & (m < MODES) & (to == d * 24 + (g - 3 * d + place[1] % 2) * MODES + m))
    parts = [mm(t, choose) for t in thirds(tall)]
    back_top[...], back_low[...] = halves(parts[0] + parts[1] + parts[2])


def put_terms(total, dots, terms):
    total = fold(total)
    total = total[:8] + total[8:] + dots
    for w in range(GRID_A):
        terms[8 * w : 8 * w + 8] = total


def pass_kernel(line, from_west, from_east, up, down):
    up[0:128] = line[0:128]
    up[128:256] = from_west[128:256]
    up[256:384] = from_east[256:384]
    down[0:128] = line[128:256]
    down[128:256] = from_west[256:384]
    down[256:384] = from_east[128:256]


def terms_kernel(
    place, ahead, back, line, from_west, from_east, from_lower, from_upper, gather, dots, token, spread, terms
):
    total = jnp.zeros((16, 2 * LOADS), F32)
    for p, q in enumerate(ORDER):
        own = (ahead, back, line)[p // 3][rows(p % 3), :]
        source, i = {
            0: (from_east, 0),
            4: (from_west, 0),
            1: (from_upper, 0),
            7: (from_upper, 1),
            2: (from_upper, 2),
            5: (from_lower, 0),
            6: (from_lower, 1),
            3: (from_lower, 2),
        }[q]
        value = (own - source[rows(i), :]) * valid_of(place, q)
        spread[rows(p), :] = value
        total += mm(gather[:, rows(p)], jnp.concatenate(halves(value), axis=1))
    put_terms(total, dots[...], terms)


def solve_kernel(terms, inverse, *outs):
    out = jnp.dot(inverse[...], terms[...], precision=HIGH, preferred_element_type=F32)
    for j in range(CHIPS):
        outs[j][...] = out[PART * j : PART * j + PART]


def sum_kernel(*refs):
    refs[-1][...] = (refs[0][...] + refs[1][...]) + (refs[2][...] + refs[3][...])


def apply_kernel(kind, *refs):
    place, share, other, back_top, back_low, pick, put, top, low, spread = refs[:10]
    rest = refs[10:]
    old = None
    if kind in ("residual", "search"):
        old, past = rest[:2]
        rest = rest[2:]
    if kind == "residual":
        lam, resid, search = rest[:3]
        rest = rest[3:]
    ahead, back, line, field, total, dots = rest[:6]
    rest = rest[6:]
    if kind == "residual":
        lam_out, resid_out = rest[:2]
        rest = rest[2:]
    left, right = rest

    y = share[...] + other[...]
    inner = y[72:73]
    total[...] = jnp.broadcast_to(inner, (8, LOADS))
    yt, yl = halves(jnp.concatenate([y, jnp.zeros((128 - PART, LOADS), F32)], axis=0))
    both = jnp.concatenate([yt, yl], axis=1)
    if kind == "residual":
        factor = past[0:1] / inner
        for q in range(4):
            p = AT[q]
            v = valid_of(place, q)
            lam_out[rows(q), :] = lam[0, q] * v + factor * search[rows(p), :]
            resid_out[rows(q), :] = resid[0, q] * v - factor * spread[rows(p), :]
    if kind == "search":
        factor = inner / past[0:1]

    blocks = [slice(256 * c, 256 * c + 256) for c in range(4)]
    for block in blocks:
        f = spread[block, :] - (fold(mm(back_top[block, :], both)) + mm(back_low[block, :], yt))
        if kind == "residual":
            f = old[block, :] - factor * f
        if kind == "search":
            f = f + factor * old[block, :]
        field[block, :] = f
        left[block, :] = jnp.concatenate(halves(f), axis=1)
    for block in blocks:
        right[block, :] = mm(pick[block, :], left[...]).astype(BF16)
    for block in blocks:
        u = fold(mm(top[block, :], right[...])) + mm(low[block, :], right[:, :LOADS])
        left[block, :] = jnp.concatenate(halves(u), axis=1)
    inner = jnp.zeros((1, LOADS), F32)
    for c, block in enumerate(blocks):
        u = fold(mm(put[block, :], left[...]))
        inner = inner + jnp.sum(u * field[block, :], axis=0, keepdims=True)
        for h in range(2):
            p = 2 * c + h
            (ahead, back, line)[p // 3][rows(p % 3), :] = u[rows(h)]
    row = iota(dots.shape, 0) & 7
    dots[...] = jnp.where(row == 6, inner, 0.0)


def last_pass_kernel(line, from_east, up, down):
    up[...] = from_east[256:384]
    down[0:128] = line[128:256]
    down[128:256] = from_east[128:256]


def last_dots_kernel(gathered, out):
    total = gathered[0:8]
    for w in range(1, 16):
        total = total + gathered[8 * w : 8 * w + 8]
    for n in range(16):
        out[8 * n : 8 * n + 8] = total


def finish_kernel(
    place, shares, lam, resid, search, gamma, ahead, line, from_east, from_lower, from_upper, lam_out, resid_out
):
    energy = shares[0:8]
    for n in range(1, 16):
        energy = energy + shares[8 * n : 8 * n + 8]
    step = gamma[0:1] / energy[6:7]
    for q, own, facing in (
        (0, ahead[0:128], from_east[0:128]),
        (1, line[0:128], from_upper[0:128]),
        (2, ahead[128:256], from_upper[128:256]),
        (3, ahead[256:384], from_lower[...]),
    ):
        lam_out[0, q] = lam[rows(q), :] + step * search[rows(AT[q]), :]
        resid_out[0, q] = resid[rows(q), :] - step * (valid_of(place, q) * (own - facing))


def per_device(
    multipliers,
    residual_in,
    flexibility,
    stiffness,
    body_modes,
    mode_counts,
    iface_index,
    coarse_inv,
):
    place = jnp.stack([lax.axis_index("wide"), lax.axis_index("narrow")]).astype(jnp.int32)
    square = ((IFACE, IFACE), BF16)
    field = ((IFACE, LOADS), F32)
    three = ((3 * SLOT, LOADS), F32)
    two = ((2 * SLOT, LOADS), F32)
    one = ((SLOT, LOADS), F32)
    few = ((8, LOADS), F32)
    thin = ((24, LOADS), F32)
    terms_shape = ((GRID_A * 8, LOADS), F32)
    index = iface_index.reshape(8, SLOT)
    stream = [pltpu.VMEM((IFACE, IFACE), F32), pltpu.SemaphoreType.DMA((4,))]

    def solve(terms, inverse):
        terms = exchange(terms, "wide")
        parts = call(solve_kernel, [((PART, LOADS), F32)] * CHIPS, terms, inverse)
        parts = [parts[0]] + [shift(parts[j], "narrow", 2 * j) for j in range(1, CHIPS)]
        share = call(sum_kernel, [((PART, LOADS), F32)], *parts)[0]
        return share, lax.ppermute(share, "narrow", [(i, i ^ 1) for i in range(GRID_B)])

    from_west = shift(residual_in, "wide", 1)
    mode_slots, ahead, back, window = call(
        prepare_kernel,
        [((8, IFACE), F32), thin, thin, ((256, 256), F32)],
        place,
        mode_counts,
        index,
        body_modes.reshape(8 * MODES, SLOT),
        coarse_inv,
        smem=(0, 1),
        far=(4,),
        scratch=[pltpu.VMEM((192, 384), F32), pltpu.SemaphoreType.DMA],
    )
    modes_west = lax.ppermute(ahead, "wide", [(i, i + 1) for i in range(GRID_A - 1)])
    modes_east = shift(back, "wide", -1)
    piece = exchange(window, "narrow")
    up, down, inverse, token = call(
        first_pass_kernel,
        [((280, LOADS), F32), ((152, LOADS), F32), ((CHIPS * PART, 256), F32), few],
        place,
        residual_in,
        from_west,
        modes_west,
        modes_east,
        mode_slots,
        piece,
        smem=(0,),
    )
    from_lower = shift(up, "narrow", 1)
    from_upper = shift(down, "narrow", -1)
    *stiff, pick, put, token = call(
        split_first_kernel,
        [square] * 4 + [few],
        token,
        index,
        stiffness,
        far=(2,),
        scratch=stream,
        bytes_moved=1 << 23,
    )
    spread, terms, back_top, back_low, gather = call(
        first_terms_kernel,
        [field, terms_shape] + [((IFACE, 128), BF16)] * 2 + [((16, IFACE), BF16)],
        place,
        residual_in,
        from_west,
        from_lower,
        from_upper,
        modes_west,
        modes_east,
        mode_slots,
        token,
        smem=(0,),
    )
    shares = solve(terms, inverse)

    def apply(kind, shares, matrix, spread, *old, last=False):
        outs = [three, three, two, field, few, ((16 * 8, LOADS), F32) if last else few]
        if kind == "residual":
            outs += [((4 * SLOT, LOADS), F32)] * 2

        def body(*refs):
            apply_kernel(kind, *refs)

        return call(
            body,
            outs,
            place,
            *shares,
            back_top,
            back_low,
            pick,
            put,
            *matrix,
            spread,
            *old,
            smem=(0,),
            scratch=[pltpu.VMEM((IFACE, 2 * LOADS), BF16)] * 2,
        )

    def coarse(ahead, back, line, dots, token):
        from_west = shift(ahead, "wide", 1)
        from_east = shift(back, "wide", -1)
        up, down = call(pass_kernel, [three, three], line, from_west, from_east)
        from_lower = shift(up, "narrow", 1)
        from_upper = shift(down, "narrow", -1)
        spread, terms = call(
            terms_kernel,
            [field, terms_shape],
            place,
            ahead,
            back,
            line,
            from_west,
            from_east,
            from_lower,
            from_upper,
            gather,
            dots,
            token,
            smem=(0,),
        )
        return solve(terms, inverse), spread

    ahead, back, line, proj, _, dots = apply("first", shares, stiff, spread)
    *flex, token = call(
        split_kernel,
        [square, square, few],
        dots,
        flexibility,
        far=(1,),
        scratch=stream,
        bytes_moved=1 << 23,
    )
    shares, spread = coarse(ahead, back, line, dots, token)
    ahead, back, line, search, gamma, dots = apply("plain", shares, flex, spread)
    shares, spread = coarse(ahead, back, line, dots, token)
    ahead, back, line, _, _, dots, lam, resid = apply(
        "residual", shares, stiff, spread, proj, gamma, multipliers, residual_in, search
    )
    shares, spread = coarse(ahead, back, line, dots, token)
    ahead, back, line, search, gamma, dots = apply(
        "search", shares, flex, spread, search, gamma, last=True
    )

    from_east = shift(back, "wide", -1)
    everywhere = ("wide", "narrow")
    gathered = exchange(dots, everywhere, LINES)
    up, down = call(last_pass_kernel, [one, two], line, from_east)
    from_lower = shift(up, "narrow", 1)
    from_upper = shift(down, "narrow", -1)
    shares = exchange(
        call(last_dots_kernel, [((16 * 8, LOADS), F32)], gathered)[0], everywhere, PLANES
    )
    out = ((1, 4, SLOT, LOADS), F32)
    return tuple(
        call(
            finish_kernel,
            [out, out],
            place,
            shares,
            lam,
            resid,
            search,
            gamma,
            ahead,
            line,
            from_east,
            from_lower,
            from_upper,
            smem=(0,),
        )
    )


def solution(mesh):
    both = ("wide", "narrow")
    in_specs = (
        P(both, None, None, None),
        P(both, None, None, None),
        P(both, None, None),
        P(both, None, None),
        P(both, None, None),
        P(both),
        P(both, None),
        P("narrow", None),
    )
    out_specs = (P(both, None, None, None), P(both, None, None, None))
    return jax.shard_map(
        per_device, mesh=mesh, in_specs=in_specs, out_specs=out_specs, check_vma=False
    )
```

```python
import jax
import jax.numpy as jnp
from jax import lax
from jax.experimental import pallas as pl
from jax.experimental.pallas import tpu as pltpu
from jax.sharding import PartitionSpec as P

GRID_A, GRID_B = 32, 8
SLOT, IFACE, MODES, LOADS = 128, 1024, 6, 128
F32, BF16 = jnp.float32, jnp.bfloat16
HIGH = lax.Precision.HIGHEST

STEP = ((1, 0), (0, 1), (1, 1), (1, -1), (-1, 0), (0, -1), (-1, -1), (-1, 1))
ORDER = (0, 2, 3, 4, 6, 7, 1, 5)
AT = {q: p for p, q in enumerate(ORDER)}
PART = 80
CHIPS = GRID_B // 2


def shift(block, axis, distance):
    size = lax.axis_size(axis)
    return lax.ppermute(block, axis, [(i, (i + distance) % size) for i in range(size)])


def exchange(block, axis, groups=None):
    return lax.all_to_all(block, axis, 0, 0, tiled=True, axis_index_groups=groups)


LINES = [[w * 8 + n for w in range(8 * y, 8 * y + 8) for n in (2 * x, 2 * x + 1)] for y in range(4) for x in range(4)]
PLANES = [[w * 8 + n for w in range(z, 32, 8) for n in range(c, 8, 2)] for z in range(8) for c in range(2)]


def call(body, outs, *args, scratch=(), smem=(), far=(), bytes_moved=None, grant=16):
    specs = [
        pl.BlockSpec(
            memory_space=pltpu.SMEM if i in smem else pltpu.HBM if i in far else pltpu.VMEM
        )
        for i in range(len(args))
    ]
    return pl.pallas_call(
        body,
        out_shape=[jax.ShapeDtypeStruct(s, d) for s, d in outs],
        in_specs=specs,
        out_specs=[pl.BlockSpec(memory_space=pltpu.VMEM)] * len(outs),
        scratch_shapes=list(scratch),
        compiler_params=pltpu.CompilerParams(vmem_limit_bytes=grant * 1024 * 1024),
        cost_estimate=None
        if bytes_moved is None
        else pl.CostEstimate(flops=0, bytes_accessed=bytes_moved, transcendentals=0),
    )(*args)


def halves(x):
    top = x.astype(BF16)
    return top, (x - top.astype(F32)).astype(BF16)


def thirds(x):
    top, rest = x.astype(BF16), None
    rest = x - top.astype(F32)
    mid = rest.astype(BF16)
    return top, mid, (rest - mid.astype(F32)).astype(BF16)


def mm(a, b):
    return jnp.dot(a, b, preferred_element_type=F32)


def mm_nt(a, b):
    return lax.dot_general(a, b, (((1,), (1,)), ((), ())), preferred_element_type=F32)


def fold(x):
    return x[:, :LOADS] + x[:, LOADS:]


def valid_of(place, q):
    a, b = place[0] + STEP[q][0], place[1] + STEP[q][1]
    return ((a >= 0) & (a < GRID_A) & (b >= 0) & (b < GRID_B)).astype(F32)


def rows(p, count=1):
    return slice(p * SLOT, (p + count) * SLOT)


def columns_of(index):
    values = index[...].astype(F32)
    return jnp.transpose(jnp.concatenate([values, jnp.zeros((SLOT - 8, SLOT), F32)], axis=0))


def iota(shape, axis):
    return lax.broadcasted_iota(jnp.int32, shape, axis)


def one_hot(condition):
    return condition.astype(F32).astype(BF16)


def steps_at(x, *bounds):
    return sum((x >= b).astype(jnp.int32) for b in bounds)


def prepare_kernel(place, counts, index, modes, inverse, mode_slots, ahead, back, window, held, arrived):
    width = GRID_A * GRID_B * MODES
    first = jnp.clip(place[0] - 1, 0, GRID_A - 3) * (GRID_B * MODES)
    start = pl.multiple_of(jnp.minimum(first // 128 * 128, width - 384), 128)
    copy = pltpu.make_async_copy(inverse.at[:, pl.ds(start, 384)], held, arrived)
    copy.start()

    keep = iota((8, SLOT), 0) < counts[0]
    pieces = []
    for j in range(8):
        own = jnp.concatenate([modes[pl.ds(j, MODES, stride=8), :], jnp.zeros((8 - MODES, SLOT), F32)], axis=0)
        a, b, c = thirds(jnp.where(keep, own, 0.0))
        pieces.append(jnp.concatenate([a, b, c, jnp.zeros((8, SLOT), BF16)], axis=0))
    stack = jnp.concatenate(pieces, axis=1)
    values = index[...].astype(F32)
    at = iota((IFACE, SLOT), 0).astype(F32)
    for p, q in enumerate(ORDER):
        part = mm(stack, one_hot(at == values[q : q + 1, :]))
        part = (part[0:8] + part[8:16] + part[16:24]) * valid_of(place, q)
        mode_slots[:, rows(p)] = part
        if p < 6:
            (ahead, back)[p // 3][8 * (p % 3) : 8 * (p % 3) + 8] = part

    copy.wait()
    choose = one_hot(iota((384, 256), 0) == iota((384, 256), 1) + (first - start))
    parts = mm(jnp.concatenate(thirds(held[...]), axis=0), choose).astype(BF16)
    wide = jnp.concatenate([parts[0:192], parts[192:384], parts[384:576]], axis=1)
    r = iota((256, 192), 0)
    source = (((r >> 3) & 3) * GRID_B + (r >> 5)) * MODES + (r & 7)
    wide = mm(one_hot((iota((256, 192), 1) == source) & ((r & 7) < MODES)), wide)
    window[...] = wide[:, :256] + wide[:, 256:512] + wide[:, 512:]


def first_pass_kernel(place, resid, from_west, modes_west, modes_east, mode_slots, up, down):
    up[0:128] = resid[0, 1]
    up[128:256] = from_west[0, 2]
    up[256:264] = mode_slots[:, rows(AT[1])]
    up[264:272] = modes_west[8:16]
    up[272:280] = modes_east[16:24]
    down[0:128] = from_west[0, 3]
    down[128:136] = mode_slots[:, rows(AT[5])]
    down[136:144] = modes_west[16:24]
    down[144:152] = modes_east[8:16]


def coarse_kernel(place, piece, inverse, token):
    token[...] = jnp.zeros((8, LOADS), F32)
    shape = (CHIPS * PART, 256)
    row, across = iota(shape, 0), iota(shape, 1)
    j = steps_at(row, PART, 2 * PART, 3 * PART)
    r = row - PART * j
    d = steps_at(r, 24, 48, 72)
    m = r - 24 * d
    offset = steps_at(m, 6, 12, 18)
    m = m - MODES * offset
    b = 2 * ((place[1] // 2 + j) & (CHIPS - 1)) - 1 + offset
    a = place[0] + d - 1
    goal = (a - jnp.clip(place[0] - 1, 0, GRID_A - 3)) * (GRID_B * MODES) + b * MODES + m
    real = (r < 72) & (b >= 0) & (b < GRID_B) & (a >= 0) & (a < GRID_A)
    parts = mm_nt(one_hot(real & (across == goal)), jnp.concatenate(thirds(piece[...]), axis=0))
    dots = ((r == 72) & ((across & 7) == 6)).astype(F32)
    inverse[...] = parts[:, :256] + parts[:, 256:512] + parts[:, 512:] + dots


def split_kernel(token, matrix, top, low, token_out, held, arrived):
    blocks = [slice(256 * c, 256 * c + 256) for c in range(4)]
    copies = [
        pltpu.make_async_copy(matrix.at[0, block, :], held.at[block, :], arrived.at[c])
        for c, block in enumerate(blocks)
    ]
    for copy in copies:
        copy.start()
    token_out[...] = token[...]
    for copy, block in zip(copies, blocks):
        copy.wait()
        top[block, :], low[block, :] = halves(held[block, :])


def split_first_kernel(token, index, matrix, top, low, pick, put, token_out, held, arrived):
    split_kernel(token, matrix, top, low, token_out, held, arrived)
    values, columns = index[...].astype(F32), columns_of(index)
    down = iota((IFACE, SLOT), 0).astype(F32)
    across = iota((SLOT, IFACE), 1).astype(F32)
    for p, q in enumerate(ORDER):
        pick[:, rows(p)] = one_hot(down == values[q : q + 1, :])
        put[rows(p), :] = one_hot(across == columns[:, q : q + 1])


def first_terms_kernel(
    place, resid, from_west, from_lower, from_upper, modes_west, modes_east, mode_slots, token,
    spread, terms, back_top, back_low, gather,
):
    own = {q: resid[0, q] for q in range(4)}
    own[4] = -from_west[0, 0]
    own[5] = -from_lower[0:128]
    own[6] = -from_lower[128:256]
    own[7] = -from_upper[0:128]
    total = jnp.zeros((16, 2 * LOADS), F32)
    for p, q in enumerate(ORDER):
        value = own[q] * valid_of(place, q)
        spread[rows(p), :] = value
        modes = jnp.concatenate(halves(mode_slots[:, rows(p)]), axis=0)
        gather[:, rows(p)] = modes
        total += mm(modes, jnp.concatenate(halves(value), axis=1))
    put_terms(total, token[...], terms)

    facing = {
        0: modes_east[0:8],
        4: modes_west[0:8],
        1: from_upper[128:136],
        7: from_upper[136:144],
        2: from_upper[144:152],
        5: from_lower[256:264],
        6: from_lower[264:272],
        3: from_lower[272:280],
    }
    nothing = jnp.zeros((8, SLOT), F32)
    columns = []
    for p, q in enumerate(ORDER):
        blocks = [nothing] * 16
        blocks[4] = mode_slots[:, rows(p)]
        blocks[(STEP[q][0] + 1) * 3 + STEP[q][1] + 1] = -facing[q] * valid_of(place, q)
        columns.append(jnp.transpose(jnp.concatenate(blocks, axis=0)))
    tall = jnp.concatenate(columns, axis=0)
    r, to = iota((128, 128), 0), iota((128, 128), 1)
    g, m = r >> 3, r & 7
    d = steps_at(g, 3, 6)
    choose = one_hot((g < 9) & (m < MODES) & (to == d * 24 + (g - 3 * d + place[1] % 2) * MODES + m))
    parts = [mm(t, choose) for t in thirds(tall)]
    back_top[...], back_low[...] = halves(parts[0] + parts[1] + parts[2])


def put_terms(total, dots, terms):
    total = fold(total)
    total = total[:8] + total[8:] + dots
    for w in range(GRID_A):
        terms[8 * w : 8 * w + 8] = total


def pass_kernel(line, from_west, from_east, up, down):
    up[0:128] = line[0:128]
    up[128:256] = from_west[128:256]
    up[256:384] = from_east[256:384]
    down[0:128] = line[128:256]
    down[128:256] = from_west[256:384]
    down[256:384] = from_east[128:256]


def terms_kernel(
    place, ahead, back, line, from_west, from_east, from_lower, from_upper, gather, dots, token, spread, terms
):
    total = jnp.zeros((16, 2 * LOADS), F32)
    for p, q in enumerate(ORDER):
        own = (ahead, back, line)[p // 3][rows(p % 3), :]
        source, i = {
            0: (from_east, 0),
            4: (from_west, 0),
            1: (from_upper, 0),
            7: (from_upper, 1),
            2: (from_upper, 2),
            5: (from_lower, 0),
            6: (from_lower, 1),
            3: (from_lower, 2),
        }[q]
        value = (own - source[rows(i), :]) * valid_of(place, q)
        spread[rows(p), :] = value
        total += mm(gather[:, rows(p)], jnp.concatenate(halves(value), axis=1))
    put_terms(total, dots[...], terms)


def solve_kernel(terms, inverse, *outs):
    out = jnp.dot(inverse[...], terms[...], precision=HIGH, preferred_element_type=F32)
    for j in range(CHIPS):
        outs[j][...] = out[PART * j : PART * j + PART]


def sum_kernel(*refs):
    refs[-1][...] = (refs[0][...] + refs[1][...]) + (refs[2][...] + refs[3][...])


def local_product(pick, put, top, low, left, right):
    blocks = [slice(256 * c, 256 * c + 256) for c in range(4)]
    for block in blocks:
        right[block, :] = mm(pick[block, :], left[...]).astype(BF16)
    for block in blocks:
        u = fold(mm(top[block, :], right[...])) + mm(low[block, :], right[:, :LOADS])
        left[block, :] = jnp.concatenate(halves(u), axis=1)
    for block in blocks:
        yield block, fold(mm(put[block, :], left[...]))


def product_kernel(token, pick, put, top, low, spread, product, left, right):
    left[...] = jnp.concatenate(halves(spread[...]), axis=1)
    for block, u in local_product(pick, put, top, low, left, right):
        product[block, :] = u


def response_kernel(token, pick, put, top, low, back_top, back_low, resp_top, resp_low, token_out, left, right):
    token_out[...] = token[...]
    left[...] = jnp.concatenate([back_top[...], back_low[...]], axis=1)
    for block, u in local_product(pick, put, top, low, left, right):
        resp_top[block, :], resp_low[block, :] = halves(u)


def coarse_part(share, other):
    y = share[...] + other[...]
    inner = y[72:73]
    yt, yl = halves(jnp.concatenate([y, jnp.zeros((128 - PART, LOADS), F32)], axis=0))
    return inner, yt, jnp.concatenate([yt, yl], axis=1)


def put_dots(inner, dots):
    row = iota(dots.shape, 0) & 7
    dots[...] = jnp.where(row == 6, inner, 0.0)


def apply_kernel(
    place, share, other, back_top, back_low, pick, put, top, low, spread,
    ahead, back, line, field, dots, left, right,
):
    _, yt, both = coarse_part(share, other)
    for c in range(4):
        block = slice(256 * c, 256 * c + 256)
        f = spread[block, :] - (fold(mm(back_top[block, :], both)) + mm(back_low[block, :], yt))
        field[block, :] = f
        left[block, :] = jnp.concatenate(halves(f), axis=1)
    inner = jnp.zeros((1, LOADS), F32)
    for c, (block, u) in enumerate(local_product(pick, put, top, low, left, right)):
        inner = inner + jnp.sum(u * field[block, :], axis=0, keepdims=True)
        for h in range(2):
            p = 2 * c + h
            (ahead, back, line)[p // 3][rows(p % 3), :] = u[rows(h)]
    put_dots(inner, dots)


def update_kernel(kind, *refs):
    place, share, other, back_top, back_low, resp_top, resp_low, product, spread = refs[:9]
    rest = refs[9:]
    if kind != "plain":
        old, old_ahead, old_back, old_line, past = rest[:5]
        rest = rest[5:]
    if kind == "residual":
        lam, resid, search = rest[:3]
        rest = rest[3:]
    ahead, back, line, dots = rest[:4]
    inner, yt, both = coarse_part(share, other)
    if kind == "residual":
        lam_out, resid_out = rest[4:]
    else:
        field, total = rest[4:]
        total[...] = jnp.broadcast_to(inner, (8, LOADS))
    if kind == "residual":
        factor = past[0:1] / inner
    if kind == "search":
        factor = inner / past[0:1]
    inner = jnp.zeros((1, LOADS), F32)
    for p, q in enumerate(ORDER):
        at = rows(p)
        f = spread[at, :] - (fold(mm(back_top[at, :], both)) + mm(back_low[at, :], yt))
        u = product[at, :] - (fold(mm(resp_top[at, :], both)) + mm(resp_low[at, :], yt))
        if kind != "plain":
            past_u = (old_ahead, old_back, old_line)[p // 3][rows(p % 3), :]
        if kind == "residual":
            if q < 4:
                v = valid_of(place, q)
                lam_out[rows(q), :] = lam[0, q] * v + factor * search[at, :]
                resid_out[rows(q), :] = resid[0, q] * v - factor * spread[at, :]
            f = old[at, :] - factor * f
            u = past_u - factor * u
        if kind == "search":
            f = f + factor * old[at, :]
            u = u + factor * past_u
        if kind != "residual":
            field[at, :] = f
        (ahead, back, line)[p // 3][rows(p % 3), :] = u
        inner = inner + jnp.sum(u * f, axis=0, keepdims=True)
    put_dots(inner, dots)


def last_pass_kernel(line, from_east, up, down):
    up[...] = from_east[256:384]
    down[0:128] = line[128:256]
    down[128:256] = from_east[128:256]


def last_dots_kernel(gathered, out):
    total = gathered[0:8]
    for w in range(1, 16):
        total = total + gathered[8 * w : 8 * w + 8]
    for n in range(16):
        out[8 * n : 8 * n + 8] = total


def finish_kernel(
    place, shares, lam, resid, search, gamma, ahead, line, from_east, from_lower, from_upper, lam_out, resid_out
):
    energy = shares[0:8]
    for n in range(1, 16):
        energy = energy + shares[8 * n : 8 * n + 8]
    step = gamma[0:1] / energy[6:7]
    for q, own, facing in (
        (0, ahead[0:128], from_east[0:128]),
        (1, line[0:128], from_upper[0:128]),
        (2, ahead[128:256], from_upper[128:256]),
        (3, ahead[256:384], from_lower[...]),
    ):
        lam_out[0, q] = lam[rows(q), :] + step * search[rows(AT[q]), :]
        resid_out[0, q] = resid[rows(q), :] - step * (valid_of(place, q) * (own - facing))


def per_device(
    multipliers,
    residual_in,
    flexibility,
    stiffness,
    body_modes,
    mode_counts,
    iface_index,
    coarse_inv,
):
    place = jnp.stack([lax.axis_index("wide"), lax.axis_index("narrow")]).astype(jnp.int32)
    square = ((IFACE, IFACE), BF16)
    field = ((IFACE, LOADS), F32)
    three = ((3 * SLOT, LOADS), F32)
    two = ((2 * SLOT, LOADS), F32)
    one = ((SLOT, LOADS), F32)
    few = ((8, LOADS), F32)
    thin = ((24, LOADS), F32)
    terms_shape = ((GRID_A * 8, LOADS), F32)
    index = iface_index.reshape(8, SLOT)
    stream = [pltpu.VMEM((IFACE, IFACE), F32), pltpu.SemaphoreType.DMA((4,))]

    work = [pltpu.VMEM((IFACE, 2 * LOADS), BF16)] * 2

    def solve(terms, spread=None, matrix=None):
        terms = exchange(terms, "wide")
        parts = call(solve_kernel, [((PART, LOADS), F32)] * CHIPS, terms, inverse)
        product = ()
        if matrix is not None:
            product = call(product_kernel, [field], parts[0], pick, put, *matrix, spread, scratch=work)
        parts = [parts[0]] + [shift(parts[j], "narrow", 2 * j) for j in range(1, CHIPS)]
        share = call(sum_kernel, [((PART, LOADS), F32)], *parts, *product)[0]
        return (share, lax.ppermute(share, "narrow", [(i, i ^ 1) for i in range(GRID_B)])), product

    from_west = shift(residual_in, "wide", 1)
    mode_slots, ahead, back, window = call(
        prepare_kernel,
        [((8, IFACE), F32), thin, thin, ((256, 256), F32)],
        place,
        mode_counts,
        index,
        body_modes.reshape(8 * MODES, SLOT),
        coarse_inv,
        smem=(0, 1),
        far=(4,),
        scratch=[pltpu.VMEM((192, 384), F32), pltpu.SemaphoreType.DMA],
    )
    modes_west = lax.ppermute(ahead, "wide", [(i, i + 1) for i in range(GRID_A - 1)])
    modes_east = shift(back, "wide", -1)
    piece = exchange(window, "narrow")
    inverse, token = call(
        coarse_kernel, [((CHIPS * PART, 256), F32), few], place, piece, smem=(0,)
    )
    up, down = call(
        first_pass_kernel,
        [((280, LOADS), F32), ((152, LOADS), F32)],
        place,
        residual_in,
        from_west,
        modes_west,
        modes_east,
        mode_slots,
        smem=(0,),
    )
    from_lower = shift(up, "narrow", 1)
    from_upper = shift(down, "narrow", -1)
    *stiff, pick, put, token = call(
        split_first_kernel,
        [square] * 4 + [few],
        token,
        index,
        stiffness,
        far=(2,),
        scratch=stream,
        bytes_moved=1 << 23,
        grant=44,
    )
    spread, terms, back_top, back_low, gather = call(
        first_terms_kernel,
        [field, terms_shape] + [((IFACE, 128), BF16)] * 2 + [((16, IFACE), BF16)],
        place,
        residual_in,
        from_west,
        from_lower,
        from_upper,
        modes_west,
        modes_east,
        mode_slots,
        token,
        smem=(0,),
    )
    shares, _ = solve(terms)

    def update(kind, shares, product, spread, response, *old, last=False):
        outs = [three, three, two, ((16 * 8, LOADS), F32) if last else few]
        outs += [((4 * SLOT, LOADS), F32)] * 2 if kind == "residual" else [field, few]

        def body(*refs):
            update_kernel(kind, *refs)

        return call(
            body, outs, place, *shares, back_top, back_low, *response, *product, spread, *old, smem=(0,)
        )

    def coarse(ahead, back, line, dots, token, matrix):
        from_west = shift(ahead, "wide", 1)
        from_east = shift(back, "wide", -1)
        up, down = call(pass_kernel, [three, three], line, from_west, from_east)
        from_lower = shift(up, "narrow", 1)
        from_upper = shift(down, "narrow", -1)
        spread, terms = call(
            terms_kernel,
            [field, terms_shape],
            place,
            ahead,
            back,
            line,
            from_west,
            from_east,
            from_lower,
            from_upper,
            gather,
            dots,
            token,
            smem=(0,),
        )
        return *solve(terms, spread, matrix), spread

    def response(token, matrix):
        return call(
            response_kernel,
            [((IFACE, 128), BF16)] * 2 + [few],
            token,
            pick,
            put,
            *matrix,
            back_top,
            back_low,
            scratch=work,
            bytes_moved=1 << 23,
        )

    ahead, back, line, proj, dots = call(
        apply_kernel,
        [three, three, two, field, few],
        place,
        *shares,
        back_top,
        back_low,
        pick,
        put,
        *stiff,
        spread,
        smem=(0,),
        scratch=work,
    )
    first_product = (ahead, back, line)
    *flex, token = call(
        split_kernel,
        [square, square, few],
        dots,
        flexibility,
        far=(1,),
        scratch=stream,
        bytes_moved=1 << 23,
    )
    *flex_response, token = response(token, flex)
    shares, product, spread = coarse(ahead, back, line, dots, token, flex)
    ahead, back, line, dots, search, gamma = update("plain", shares, product, spread, flex_response)
    second_product = (ahead, back, line)
    *stiff_response, token = response(dots, stiff)
    shares, product, spread = coarse(ahead, back, line, dots, token, stiff)
    ahead, back, line, dots, lam, resid = update(
        "residual", shares, product, spread, stiff_response, proj, *first_product, gamma,
        multipliers, residual_in, search,
    )
    shares, product, spread = coarse(ahead, back, line, dots, dots, flex)
    ahead, back, line, dots, search, gamma = update(
        "search", shares, product, spread, flex_response, search, *second_product, gamma, last=True
    )

    from_east = shift(back, "wide", -1)
    everywhere = ("wide", "narrow")
    gathered = exchange(dots, everywhere, LINES)
    up, down = call(last_pass_kernel, [one, two], line, from_east)
    from_lower = shift(up, "narrow", 1)
    from_upper = shift(down, "narrow", -1)
    shares = exchange(
        call(last_dots_kernel, [((16 * 8, LOADS), F32)], gathered)[0], everywhere, PLANES
    )
    out = ((1, 4, SLOT, LOADS), F32)
    return tuple(
        call(
            finish_kernel,
            [out, out],
            place,
            shares,
            lam,
            resid,
            search,
            gamma,
            ahead,
            line,
            from_east,
            from_lower,
            from_upper,
            smem=(0,),
        )
    )


def solution(mesh):
    both = ("wide", "narrow")
    in_specs = (
        P(both, None, None, None),
        P(both, None, None, None),
        P(both, None, None),
        P(both, None, None),
        P(both, None, None),
        P(both),
        P(both, None),
        P("narrow", None),
    )
    out_specs = (P(both, None, None, None), P(both, None, None, None))
    return jax.shard_map(
        per_device, mesh=mesh, in_specs=in_specs, out_specs=out_specs, check_vma=False
    )
```

```python
import jax
import jax.numpy as jnp
from jax import lax
from jax.experimental import pallas as pl
from jax.experimental.pallas import tpu as pltpu
from jax.sharding import PartitionSpec as P

GRID_A, GRID_B = 32, 8
SLOT, IFACE, MODES, LOADS = 128, 1024, 6, 128
F32, BF16 = jnp.float32, jnp.bfloat16

STEP = ((1, 0), (0, 1), (1, 1), (1, -1), (-1, 0), (0, -1), (-1, -1), (-1, 1))
ORDER = (0, 2, 3, 4, 6, 7, 1, 5)
AT = {q: p for p, q in enumerate(ORDER)}
PART = 80
CHIPS = GRID_B // 2


def shift(block, axis, distance):
    size = lax.axis_size(axis)
    return lax.ppermute(block, axis, [(i, (i + distance) % size) for i in range(size)])


def exchange(block, axis, groups=None):
    return lax.all_to_all(block, axis, 0, 0, tiled=True, axis_index_groups=groups)


LINES = [[w * 8 + n for w in range(8 * y, 8 * y + 8) for n in (2 * x, 2 * x + 1)] for y in range(4) for x in range(4)]
PLANES = [[w * 8 + n for w in range(z, 32, 8) for n in range(c, 8, 2)] for z in range(8) for c in range(2)]


def call(body, outs, *args, scratch=(), smem=(), far=(), bytes_moved=None, grant=16):
    specs = [
        pl.BlockSpec(
            memory_space=pltpu.SMEM if i in smem else pltpu.HBM if i in far else pltpu.VMEM
        )
        for i in range(len(args))
    ]
    return pl.pallas_call(
        body,
        out_shape=[jax.ShapeDtypeStruct(s, d) for s, d in outs],
        in_specs=specs,
        out_specs=[pl.BlockSpec(memory_space=pltpu.VMEM)] * len(outs),
        scratch_shapes=list(scratch),
        compiler_params=pltpu.CompilerParams(vmem_limit_bytes=grant * 1024 * 1024),
        cost_estimate=None
        if bytes_moved is None
        else pl.CostEstimate(flops=0, bytes_accessed=bytes_moved, transcendentals=0),
    )(*args)


def halves(x):
    top = x.astype(BF16)
    return top, (x - top.astype(F32)).astype(BF16)


def thirds(x):
    top, rest = x.astype(BF16), None
    rest = x - top.astype(F32)
    mid = rest.astype(BF16)
    return top, mid, (rest - mid.astype(F32)).astype(BF16)


def mm(a, b):
    return jnp.dot(a, b, preferred_element_type=F32)


def mm_nt(a, b):
    return lax.dot_general(a, b, (((1,), (1,)), ((), ())), preferred_element_type=F32)


def fold(x):
    return x[:, :LOADS] + x[:, LOADS:]


def valid_of(place, q):
    a, b = place[0] + STEP[q][0], place[1] + STEP[q][1]
    return ((a >= 0) & (a < GRID_A) & (b >= 0) & (b < GRID_B)).astype(F32)


def rows(p, count=1):
    return slice(p * SLOT, (p + count) * SLOT)


def columns_of(index):
    values = index[...].astype(F32)
    return jnp.transpose(jnp.concatenate([values, jnp.zeros((SLOT - 8, SLOT), F32)], axis=0))


def iota(shape, axis):
    return lax.broadcasted_iota(jnp.int32, shape, axis)


def one_hot(condition):
    return condition.astype(F32).astype(BF16)


def steps_at(x, *bounds):
    return sum((x >= b).astype(jnp.int32) for b in bounds)


def prepare_kernel(place, counts, index, modes, inverse, mode_slots, ahead, back, window, held, arrived):
    width = GRID_A * GRID_B * MODES
    first = jnp.clip(place[0] - 1, 0, GRID_A - 3) * (GRID_B * MODES)
    start = pl.multiple_of(jnp.minimum(first // 128 * 128, width - 384), 128)
    copy = pltpu.make_async_copy(inverse.at[:, pl.ds(start, 384)], held, arrived)
    copy.start()

    keep = iota((8, SLOT), 0) < counts[0]
    pieces = []
    for j in range(8):
        own = jnp.concatenate([modes[pl.ds(j, MODES, stride=8), :], jnp.zeros((8 - MODES, SLOT), F32)], axis=0)
        a, b, c = thirds(jnp.where(keep, own, 0.0))
        pieces.append(jnp.concatenate([a, b, c, jnp.zeros((8, SLOT), BF16)], axis=0))
    stack = jnp.concatenate(pieces, axis=1)
    values = index[...].astype(F32)
    at = iota((IFACE, SLOT), 0).astype(F32)
    for p, q in enumerate(ORDER):
        part = mm(stack, one_hot(at == values[q : q + 1, :]))
        part = (part[0:8] + part[8:16] + part[16:24]) * valid_of(place, q)
        mode_slots[:, rows(p)] = part
        if p < 6:
            (ahead, back)[p // 3][8 * (p % 3) : 8 * (p % 3) + 8] = part

    copy.wait()
    choose = one_hot(iota((384, 256), 0) == iota((384, 256), 1) + (first - start))
    parts = mm(jnp.concatenate(thirds(held[...]), axis=0), choose).astype(BF16)
    wide = jnp.concatenate([parts[0:192], parts[192:384], parts[384:576]], axis=1)
    r = iota((256, 192), 0)
    source = (((r >> 3) & 3) * GRID_B + (r >> 5)) * MODES + (r & 7)
    wide = mm(one_hot((iota((256, 192), 1) == source) & ((r & 7) < MODES)), wide)
    window[...] = wide[:, :256] + wide[:, 256:512] + wide[:, 512:]


def first_pass_kernel(place, resid, from_west, modes_west, modes_east, mode_slots, up, down):
    up[0:128] = resid[0, 1]
    up[128:256] = from_west[0, 2]
    up[256:264] = mode_slots[:, rows(AT[1])]
    up[264:272] = modes_west[8:16]
    up[272:280] = modes_east[16:24]
    down[0:128] = from_west[0, 3]
    down[128:136] = mode_slots[:, rows(AT[5])]
    down[136:144] = modes_west[16:24]
    down[144:152] = modes_east[8:16]


def coarse_kernel(place, piece, inverse, token):
    token[...] = jnp.zeros((8, LOADS), F32)
    shape = (CHIPS * PART, 256)
    row, across = iota(shape, 0), iota(shape, 1)
    j = steps_at(row, PART, 2 * PART, 3 * PART)
    r = row - PART * j
    d = steps_at(r, 24, 48, 72)
    m = r - 24 * d
    offset = steps_at(m, 6, 12, 18)
    m = m - MODES * offset
    b = 2 * ((place[1] // 2 + j) & (CHIPS - 1)) - 1 + offset
    a = place[0] + d - 1
    goal = (a - jnp.clip(place[0] - 1, 0, GRID_A - 3)) * (GRID_B * MODES) + b * MODES + m
    real = (r < 72) & (b >= 0) & (b < GRID_B) & (a >= 0) & (a < GRID_A)
    parts = mm_nt(one_hot(real & (across == goal)), jnp.concatenate(thirds(piece[...]), axis=0))
    dots = ((r == 72) & ((across & 7) == 6)).astype(F32)
    inverse[...] = parts[:, :256] + parts[:, 256:512] + parts[:, 512:] + dots


def split_kernel(token, matrix, top, low, token_out, held, arrived):
    blocks = [slice(256 * c, 256 * c + 256) for c in range(4)]
    copies = [
        pltpu.make_async_copy(matrix.at[0, block, :], held.at[block, :], arrived.at[c])
        for c, block in enumerate(blocks)
    ]
    for copy in copies:
        copy.start()
    token_out[...] = token[...]
    for c, copy in enumerate(copies):
        copy.wait()

        @pl.loop(0, 8)
        def _(k):
            block = pl.ds(pl.multiple_of(256 * c + 32 * k, 32), 32)
            top[block, :], low[block, :] = halves(held[block, :])


def split_first_kernel(token, index, matrix, top, low, pick, put, token_out, held, arrived):
    split_kernel(token, matrix, top, low, token_out, held, arrived)
    values, columns = index[...].astype(F32), columns_of(index)

    @pl.loop(0, 8)
    def _(k):
        start = pl.multiple_of(SLOT * k, SLOT)
        block, base = pl.ds(start, SLOT), start.astype(F32)
        down = iota((SLOT, SLOT), 0).astype(F32) + base
        across = iota((SLOT, SLOT), 1).astype(F32) + base
        for p, q in enumerate(ORDER):
            pick[block, rows(p)] = one_hot(down == values[q : q + 1, :])
            put[rows(p), block] = one_hot(across == columns[:, q : q + 1])


def first_terms_kernel(
    place, resid, from_west, from_lower, from_upper, modes_west, modes_east, mode_slots, token,
    spread, terms, back_top, back_low, gather,
):
    own = {q: resid[0, q] for q in range(4)}
    own[4] = -from_west[0, 0]
    own[5] = -from_lower[0:128]
    own[6] = -from_lower[128:256]
    own[7] = -from_upper[0:128]
    total = jnp.zeros((16, 2 * LOADS), F32)
    for p, q in enumerate(ORDER):
        value = own[q] * valid_of(place, q)
        spread[rows(p), :] = value
        modes = jnp.concatenate(halves(mode_slots[:, rows(p)]), axis=0)
        gather[:, rows(p)] = modes
        total += mm(modes, jnp.concatenate(halves(value), axis=1))
    put_terms(total, token[...], terms)

    facing = {
        0: modes_east[0:8],
        4: modes_west[0:8],
        1: from_upper[128:136],
        7: from_upper[136:144],
        2: from_upper[144:152],
        5: from_lower[256:264],
        6: from_lower[264:272],
        3: from_lower[272:280],
    }
    nothing = jnp.zeros((8, SLOT), F32)
    columns = []
    for p, q in enumerate(ORDER):
        blocks = [nothing] * 16
        blocks[4] = mode_slots[:, rows(p)]
        blocks[(STEP[q][0] + 1) * 3 + STEP[q][1] + 1] = -facing[q] * valid_of(place, q)
        columns.append(jnp.transpose(jnp.concatenate(blocks, axis=0)))
    tall = jnp.concatenate(columns, axis=0)
    r, to = iota((128, 128), 0), iota((128, 128), 1)
    g, m = r >> 3, r & 7
    d = steps_at(g, 3, 6)
    choose = one_hot((g < 9) & (m < MODES) & (to == d * 24 + (g - 3 * d + place[1] % 2) * MODES + m))
    parts = [mm(t, choose) for t in thirds(tall)]
    back_top[...], back_low[...] = halves(parts[0] + parts[1] + parts[2])


def put_terms(total, dots, terms):
    total = fold(total)
    total = total[:8] + total[8:] + dots
    for w in range(GRID_A):
        terms[8 * w : 8 * w + 8] = total


def pass_kernel(line, from_west, from_east, up, down):
    up[0:128] = line[0:128]
    up[128:256] = from_west[128:256]
    up[256:384] = from_east[256:384]
    down[0:128] = line[128:256]
    down[128:256] = from_west[256:384]
    down[256:384] = from_east[128:256]


def terms_kernel(
    place, ahead, back, line, from_west, from_east, from_lower, from_upper, gather, dots, token, spread, terms
):
    total = jnp.zeros((16, 2 * LOADS), F32)
    for p, q in enumerate(ORDER):
        own = (ahead, back, line)[p // 3][rows(p % 3), :]
        source, i = {
            0: (from_east, 0),
            4: (from_west, 0),
            1: (from_upper, 0),
            7: (from_upper, 1),
            2: (from_upper, 2),
            5: (from_lower, 0),
            6: (from_lower, 1),
            3: (from_lower, 2),
        }[q]
        value = (own - source[rows(i), :]) * valid_of(place, q)
        spread[rows(p), :] = value
        total += mm(gather[:, rows(p)], jnp.concatenate(halves(value), axis=1))
    put_terms(total, dots[...], terms)


def solve_kernel(terms, inverse, *outs):
    et, el = halves(terms[...])
    top, low = halves(inverse[...])
    out = fold(mm(top, jnp.concatenate([et, el], axis=1))) + mm(low, et)
    for j in range(CHIPS):
        outs[j][...] = out[PART * j : PART * j + PART]


def sum_kernel(*refs):
    refs[-1][...] = (refs[0][...] + refs[1][...]) + (refs[2][...] + refs[3][...])


def local_product(pick, put, top, low, left, right, rolled=0):
    def first(block):
        right[block, :] = mm(pick[block, :], left[...]).astype(BF16)

    def second(block):
        u = fold(mm(top[block, :], right[...])) + mm(low[block, :], right[:, :LOADS])
        left[block, :] = jnp.concatenate(halves(u), axis=1)

    blocks = [slice(256 * c, 256 * c + 256) for c in range(4)]
    for part in (first, second):
        if rolled:
            size = IFACE // rolled
            pl.loop(0, rolled)(lambda c: part(pl.ds(pl.multiple_of(size * c, size), size)))
        else:
            for block in blocks:
                part(block)
    for block in blocks:
        yield block, fold(mm(put[block, :], left[...]))


def product_kernel(token, pick, put, top, low, spread, product, left, right):
    left[...] = jnp.concatenate(halves(spread[...]), axis=1)
    for block, u in local_product(pick, put, top, low, left, right):
        product[block, :] = u


def response_kernel(token, pick, put, top, low, back_top, back_low, resp_top, resp_low, token_out, left, right):
    token_out[...] = token[...]
    left[...] = jnp.concatenate([back_top[...], back_low[...]], axis=1)
    for block, u in local_product(pick, put, top, low, left, right, rolled=4):
        resp_top[block, :], resp_low[block, :] = halves(u)


def coarse_part(share, other):
    y = share[...] + other[...]
    inner = y[72:73]
    yt, yl = halves(jnp.concatenate([y, jnp.zeros((128 - PART, LOADS), F32)], axis=0))
    return inner, yt, jnp.concatenate([yt, yl], axis=1)


def put_dots(inner, dots):
    row = iota(dots.shape, 0) & 7
    dots[...] = jnp.where(row == 6, inner, 0.0)


def apply_kernel(
    place, share, other, back_top, back_low, pick, put, top, low, spread,
    ahead, back, line, field, dots, left, right,
):
    _, yt, both = coarse_part(share, other)
    for c in range(4):
        block = slice(256 * c, 256 * c + 256)
        f = spread[block, :] - (fold(mm(back_top[block, :], both)) + mm(back_low[block, :], yt))
        field[block, :] = f
        left[block, :] = jnp.concatenate(halves(f), axis=1)
    inner = jnp.zeros((1, LOADS), F32)
    for c, (block, u) in enumerate(local_product(pick, put, top, low, left, right, rolled=2)):
        inner = inner + jnp.sum(u * field[block, :], axis=0, keepdims=True)
        for h in range(2):
            p = 2 * c + h
            (ahead, back, line)[p // 3][rows(p % 3), :] = u[rows(h)]
    put_dots(inner, dots)


def update_kernel(kind, *refs):
    place, share, other, back_top, back_low, resp_top, resp_low, product, spread = refs[:9]
    rest = refs[9:]
    if kind != "plain":
        old, old_ahead, old_back, old_line, past = rest[:5]
        rest = rest[5:]
    if kind == "residual":
        lam, resid, search = rest[:3]
        rest = rest[3:]
    ahead, back, line, dots = rest[:4]
    inner, yt, both = coarse_part(share, other)
    if kind == "residual":
        lam_out, resid_out = rest[4:]
    else:
        field, total = rest[4:]
        total[...] = jnp.broadcast_to(inner, (8, LOADS))
    if kind == "residual":
        factor = past[0:1] / inner
    if kind == "search":
        factor = inner / past[0:1]
    inner = jnp.zeros((1, LOADS), F32)
    for p, q in enumerate(ORDER):
        at = rows(p)
        f = spread[at, :] - (fold(mm(back_top[at, :], both)) + mm(back_low[at, :], yt))
        u = product[at, :] - (fold(mm(resp_top[at, :], both)) + mm(resp_low[at, :], yt))
        if kind != "plain":
            past_u = (old_ahead, old_back, old_line)[p // 3][rows(p % 3), :]
        if kind == "residual":
            if q < 4:
                v = valid_of(place, q)
                lam_out[rows(q), :] = lam[0, q] * v + factor * search[at, :]
                resid_out[rows(q), :] = resid[0, q] * v - factor * spread[at, :]
            f = old[at, :] - factor * f
            u = past_u - factor * u
        if kind == "search":
            f = f + factor * old[at, :]
            u = u + factor * past_u
        if kind != "residual":
            field[at, :] = f
        (ahead, back, line)[p // 3][rows(p % 3), :] = u
        inner = inner + jnp.sum(u * f, axis=0, keepdims=True)
    put_dots(inner, dots)


def last_pass_kernel(line, from_east, up, down):
    up[...] = from_east[256:384]
    down[0:128] = line[128:256]
    down[128:256] = from_east[128:256]


def last_dots_kernel(gathered, out):
    total = gathered[0:8]
    for w in range(1, 16):
        total = total + gathered[8 * w : 8 * w + 8]
    for n in range(16):
        out[8 * n : 8 * n + 8] = total


def finish_kernel(
    place, shares, lam, resid, search, gamma, ahead, line, from_east, from_lower, from_upper, lam_out, resid_out
):
    energy = shares[0:8]
    for n in range(1, 16):
        energy = energy + shares[8 * n : 8 * n + 8]
    step = gamma[0:1] / energy[6:7]
    for q, own, facing in (
        (0, ahead[0:128], from_east[0:128]),
        (1, line[0:128], from_upper[0:128]),
        (2, ahead[128:256], from_upper[128:256]),
        (3, ahead[256:384], from_lower[...]),
    ):
        lam_out[0, q] = lam[rows(q), :] + step * search[rows(AT[q]), :]
        resid_out[0, q] = resid[rows(q), :] - step * (valid_of(place, q) * (own - facing))


def per_device(
    multipliers,
    residual_in,
    flexibility,
    stiffness,
    body_modes,
    mode_counts,
    iface_index,
    coarse_inv,
):
    place = jnp.stack([lax.axis_index("wide"), lax.axis_index("narrow")]).astype(jnp.int32)
    square = ((IFACE, IFACE), BF16)
    field = ((IFACE, LOADS), F32)
    three = ((3 * SLOT, LOADS), F32)
    two = ((2 * SLOT, LOADS), F32)
    one = ((SLOT, LOADS), F32)
    few = ((8, LOADS), F32)
    thin = ((24, LOADS), F32)
    terms_shape = ((GRID_A * 8, LOADS), F32)
    index = iface_index.reshape(8, SLOT)
    stream = [pltpu.VMEM((IFACE, IFACE), F32), pltpu.SemaphoreType.DMA((4,))]

    work = [pltpu.VMEM((IFACE, 2 * LOADS), BF16)] * 2

    def solve(terms, spread=None, matrix=None):
        terms = exchange(terms, "wide")
        parts = call(solve_kernel, [((PART, LOADS), F32)] * CHIPS, terms, inverse)
        product = ()
        if matrix is not None:
            product = call(product_kernel, [field], parts[0], pick, put, *matrix, spread, scratch=work)
        parts = [parts[0]] + [shift(parts[j], "narrow", 2 * j) for j in range(1, CHIPS)]
        share = call(sum_kernel, [((PART, LOADS), F32)], *parts, *product)[0]
        return (share, lax.ppermute(share, "narrow", [(i, i ^ 1) for i in range(GRID_B)])), product

    from_west = shift(residual_in, "wide", 1)
    mode_slots, ahead, back, window = call(
        prepare_kernel,
        [((8, IFACE), F32), thin, thin, ((256, 256), F32)],
        place,
        mode_counts,
        index,
        body_modes.reshape(8 * MODES, SLOT),
        coarse_inv,
        smem=(0, 1),
        far=(4,),
        scratch=[pltpu.VMEM((192, 384), F32), pltpu.SemaphoreType.DMA],
    )
    modes_west = lax.ppermute(ahead, "wide", [(i, i + 1) for i in range(GRID_A - 1)])
    modes_east = shift(back, "wide", -1)
    piece = exchange(window, "narrow")
    inverse, token = call(
        coarse_kernel, [((CHIPS * PART, 256), F32), few], place, piece, smem=(0,)
    )
    up, down = call(
        first_pass_kernel,
        [((280, LOADS), F32), ((152, LOADS), F32)],
        place,
        residual_in,
        from_west,
        modes_west,
        modes_east,
        mode_slots,
        smem=(0,),
    )
    from_lower = shift(up, "narrow", 1)
    from_upper = shift(down, "narrow", -1)
    *stiff, pick, put, token = call(
        split_first_kernel,
        [square] * 4 + [few],
        token,
        index,
        stiffness,
        far=(2,),
        scratch=stream,
        bytes_moved=1 << 23,
        grant=44,
    )
    spread, terms, back_top, back_low, gather = call(
        first_terms_kernel,
        [field, terms_shape] + [((IFACE, 128), BF16)] * 2 + [((16, IFACE), BF16)],
        place,
        residual_in,
        from_west,
        from_lower,
        from_upper,
        modes_west,
        modes_east,
        mode_slots,
        token,
        smem=(0,),
    )
    shares, _ = solve(terms)

    def update(kind, shares, product, spread, response, *old, last=False):
        outs = [three, three, two, ((16 * 8, LOADS), F32) if last else few]
        outs += [((4 * SLOT, LOADS), F32)] * 2 if kind == "residual" else [field, few]

        def body(*refs):
            update_kernel(kind, *refs)

        return call(
            body, outs, place, *shares, back_top, back_low, *response, *product, spread, *old, smem=(0,)
        )

    def coarse(ahead, back, line, dots, token, matrix):
        from_west = shift(ahead, "wide", 1)
        from_east = shift(back, "wide", -1)
        up, down = call(pass_kernel, [three, three], line, from_west, from_east)
        from_lower = shift(up, "narrow", 1)
        from_upper = shift(down, "narrow", -1)
        spread, terms = call(
            terms_kernel,
            [field, terms_shape],
            place,
            ahead,
            back,
            line,
            from_west,
            from_east,
            from_lower,
            from_upper,
            gather,
            dots,
            token,
            smem=(0,),
        )
        return *solve(terms, spread, matrix), spread

    def response(token, matrix):
        return call(
            response_kernel,
            [((IFACE, 128), BF16)] * 2 + [few],
            token,
            pick,
            put,
            *matrix,
            back_top,
            back_low,
            scratch=work,
            bytes_moved=1 << 23,
        )

    ahead, back, line, proj, dots = call(
        apply_kernel,
        [three, three, two, field, few],
        place,
        *shares,
        back_top,
        back_low,
        pick,
        put,
        *stiff,
        spread,
        smem=(0,),
        scratch=work,
    )
    first_product = (ahead, back, line)
    *flex, token = call(
        split_kernel,
        [square, square, few],
        dots,
        flexibility,
        far=(1,),
        scratch=stream,
        bytes_moved=1 << 23,
    )
    *flex_response, token = response(token, flex)
    shares, product, spread = coarse(ahead, back, line, dots, token, flex)
    ahead, back, line, dots, search, gamma = update("plain", shares, product, spread, flex_response)
    second_product = (ahead, back, line)
    *stiff_response, token = response(dots, stiff)
    shares, product, spread = coarse(ahead, back, line, dots, token, stiff)
    ahead, back, line, dots, lam, resid = update(
        "residual", shares, product, spread, stiff_response, proj, *first_product, gamma,
        multipliers, residual_in, search,
    )
    shares, product, spread = coarse(ahead, back, line, dots, dots, flex)
    ahead, back, line, dots, search, gamma = update(
        "search", shares, product, spread, flex_response, search, *second_product, gamma, last=True
    )

    from_east = shift(back, "wide", -1)
    everywhere = ("wide", "narrow")
    gathered = exchange(dots, everywhere, LINES)
    up, down = call(last_pass_kernel, [one, two], line, from_east)
    from_lower = shift(up, "narrow", 1)
    from_upper = shift(down, "narrow", -1)
    shares = exchange(
        call(last_dots_kernel, [((16 * 8, LOADS), F32)], gathered)[0], everywhere, PLANES
    )
    out = ((1, 4, SLOT, LOADS), F32)
    return tuple(
        call(
            finish_kernel,
            [out, out],
            place,
            shares,
            lam,
            resid,
            search,
            gamma,
            ahead,
            line,
            from_east,
            from_lower,
            from_upper,
            smem=(0,),
        )
    )


def solution(mesh):
    both = ("wide", "narrow")
    in_specs = (
        P(both, None, None, None),
        P(both, None, None, None),
        P(both, None, None),
        P(both, None, None),
        P(both, None, None),
        P(both),
        P(both, None),
        P("narrow", None),
    )
    out_specs = (P(both, None, None, None), P(both, None, None, None))
    return jax.shard_map(
        per_device, mesh=mesh, in_specs=in_specs, out_specs=out_specs, check_vma=False
    )
```
